32 devices in a mesh: gx: 4 (over z), gy: 8 (over y, x, core).
Axes of the slice: x: 2, y: 2, z: 4, core: 2. Of those that a mesh axis runs over, the one named last changes fastest.
Arguments:
- tokens: bfloat16 [2, 128, 18432], P(None, 'gy', 'gx'), may hold values from -250 to 250
- norm_gain: float32 [18432], P('gx'), may hold values from 0.25 to 1.75
- w_query: bfloat16 [18432, 12288], P('gx', 'gy'), may hold values from -0.046875 to 0.046875
- w_kv: bfloat16 [18432, 512], P('gx'), may hold values from -0.046875 to 0.046875
- w_out: bfloat16 [12288, 18432], P('gy', 'gx'), may hold values from -0.0546875 to 0.0546875
- cache_keys: bfloat16 [128, 2048, 256], P(('gx', 'gy')), may hold values from -1000 to 1000
- cache_values: bfloat16 [128, 2048, 256], P(('gx', 'gy')), may hold values from -6 to 6
- lengths: int32 [128], P(('gx', 'gy')), may hold values from 1024 to 2048, as said below
Outputs:
- attn_branch: bfloat16 [2, 128, 18432], P(None, 'gy', 'gx')
The draws below stay inside these ranges and needn't reach their ends.
Inputs may be any that keep to these rules, and one draw needn't show every extreme that they name: `lengths`: each row's valid cache length; some row holds exactly 2048 and some exactly 1024.
All inputs are finite; a program needn't handle non-finite values.
Results may differ from the reference program's by a relative error of at most 0.02.
The reference program's roundings to bfloat16 on the way count: a program that leaves them out, or rounds other values in their place, can miss the bound.
Values may be sent and summed in bfloat16 or wider, within the bound.
A program may use at most 128 MiB of HBM per device.

```python
import math
import jax
import jax.numpy as jnp
from jax import lax

D = 18432
HEADS = 48
HEAD_DIM = 256
CACHE = 2048
BATCH = 128
N_GY = 8


def draw_tokens(key, part):
    key = jax.random.fold_in(key, 11)
    key_base, key_rows = jax.random.split(key, 2)
    row_scale = jnp.exp(jax.random.uniform(key_rows, (2, BATCH, 1), jnp.float32, 0.0, math.log(10.0)))
    base_vals = jnp.clip(jax.random.normal(key_base, (2, BATCH, D), jnp.float32), -6.0, 6.0)
    growth = math.log(3.0)
    column_scale = jnp.exp(growth * jnp.arange(D, dtype=jnp.float32) / (D - 1))
    return (base_vals * row_scale * column_scale[None, None, :]).astype(jnp.bfloat16)


def draw_cache_keys(key, part):
    key = jax.random.fold_in(key, 23)
    key_base = jax.random.fold_in(key, 0)
    base_vals = jnp.clip(jax.random.normal(key_base, (BATCH, CACHE, HEAD_DIM), jnp.float32), -6.0, 6.0)
    keys_out = base_vals
    return keys_out.astype(jnp.bfloat16)


def draw_lengths(key, part):
    key = jax.random.fold_in(key, 37)
    key_lens, key_first, key_offset = jax.random.split(key, 3)
    lens_out = jax.random.randint(key_lens, (BATCH,), CACHE // 2, CACHE + 1)
    first_row = jax.random.randint(key_first, (), 0, BATCH)
    other_row = (first_row + 1 + jax.random.randint(key_offset, (), 0, BATCH - 1)) % BATCH
    lens_out = lens_out.at[first_row].set(CACHE)
    lens_out = lens_out.at[other_row].set(CACHE // 2)
    return lens_out.astype(jnp.int32)


def levels(key, dims, shards, least, high):
    level = 1.0
    for axis_at, shards_of in shards:
        draws = jax.random.uniform(jax.random.fold_in(jax.random.fold_in(key, 6), axis_at), (shards_of,), jnp.float32, least / len(shards), high / len(shards))
        level = level * jnp.repeat(jnp.exp(draws), dims[axis_at] // shards_of).reshape((-1,) + (1,) * (len(dims) - 1 - axis_at))
    return level


def bell_draw(rng, extent, scale, limit, pieces=(), held_as=jnp.bfloat16):
    entries = jax.random.normal(rng, extent, jnp.float32) * scale
    if len(pieces) > 0:
        entries = levels(rng, extent, pieces, -0.22, 0.18) * entries
    return jnp.clip(entries, min=-limit, max=limit).astype(held_as)


def setup_inputs(seed: int = 0) -> dict:
    key_of = jax.random.split(jax.random.key(seed), 9)
    return {
        "tokens": draw_tokens(jax.random.fold_in(key_of[8], 71), 0),
        "norm_gain": jnp.clip(1.0 + 0.15 * jax.random.normal(key_of[1], (D,), jnp.float32), 0.25, 1.75),
        "w_query": bell_draw(key_of[2], (D, HEADS * HEAD_DIM), D ** -0.5, 0.046875, ((0, 4), (1, 8))),
        "w_kv": bell_draw(key_of[3], (D, 2 * HEAD_DIM), D ** -0.5, 0.046875, ((0, 4),)),
        "w_out": bell_draw(key_of[4], (HEADS * HEAD_DIM, D), (HEADS * HEAD_DIM) ** -0.5, 0.0546875, ((0, 8), (1, 4))),
        "cache_keys": draw_cache_keys(jax.random.fold_in(key_of[8], 71), 0),
        "cache_values": bell_draw(key_of[6], (BATCH, CACHE, HEAD_DIM), 1.0, 6.0, ((0, 32),)),
        "lengths": draw_lengths(jax.random.fold_in(key_of[8], 71), 0),
    }


def layer_norm(inputs, gain_vec):
    values_f = inputs.astype(jnp.float32)
    average = lax.optimization_barrier(jnp.mean(values_f, axis=-1, keepdims=True))
    centred = values_f - average
    spread = lax.optimization_barrier(jnp.mean(centred * centred, axis=-1, keepdims=True))
    return (centred * lax.rsqrt(spread + 1e-05) * gain_vec.astype(jnp.float32)).astype(jnp.bfloat16)

def attend(query, keys_all, values_all, lens_here, new_keys, new_values):
    factor = query.shape[-1] ** (-0.5)
    query_f = query.astype(jnp.float32)
    scores_c = jnp.einsum('rhd,rld->rhl', query_f, keys_all.astype(jnp.float32)) * factor
    position = jnp.arange(keys_all.shape[1], dtype=jnp.int32)
    usable = position[None, None, :] < lens_here.astype(jnp.int32)[:, None, None]
    scores_c = jnp.where(usable, scores_c, -1e+30)
    scores_n = jnp.einsum('rhd,rsd->rhs', query_f, new_keys.astype(jnp.float32)) * factor
    highest = jnp.maximum(lax.optimization_barrier(jnp.max(scores_c, axis=-1)), lax.optimization_barrier(jnp.max(scores_n, axis=-1)))[..., None]
    exp_c = jnp.exp(scores_c - highest)
    exp_n = jnp.exp(scores_n - highest)
    totals = lax.optimization_barrier(jnp.sum(exp_c, axis=-1, keepdims=True)) + lax.optimization_barrier(jnp.sum(exp_n, axis=-1, keepdims=True))
    weight_c = (exp_c / totals).astype(jnp.bfloat16)
    weight_n = (exp_n / totals).astype(jnp.bfloat16)
    result = jnp.einsum('rhl,rld->rhd', weight_c.astype(jnp.float32), values_all.astype(jnp.float32))
    result = result + jnp.einsum('rhs,rsd->rhd', weight_n.astype(jnp.float32), new_values.astype(jnp.float32))
    return result.reshape(result.shape[0], -1).astype(jnp.bfloat16)

def grouped_output(mixed, w_out):
    cols = HEADS * HEAD_DIM // N_GY

    def add_group(index, total):
        start = (index * cols).astype(jnp.int32)
        left = lax.dynamic_slice_in_dim(mixed, start, cols, 1)
        right = lax.dynamic_slice_in_dim(w_out, start, cols, 0)
        partial_value = jnp.dot(left, right, preferred_element_type=jnp.float32).astype(jnp.bfloat16)
        return total + partial_value.astype(jnp.float32)
    start_total = jnp.zeros((mixed.shape[0], w_out.shape[1]), jnp.float32)
    return lax.fori_loop(0, N_GY, add_group, start_total).astype(jnp.bfloat16)

def reference(tokens, norm_gain, w_query, w_kv, w_out, cache_keys, cache_values, lengths):
    block_rows = math.gcd(BATCH, 64)
    blocks = BATCH // block_rows
    results = []
    kept_keys = []
    kept_values = []
    for section in range(2):
        normed = layer_norm(tokens[section], norm_gain)
        query = jnp.dot(normed, w_query, preferred_element_type=jnp.float32).astype(jnp.bfloat16)
        key_value = jnp.dot(normed, w_kv, preferred_element_type=jnp.float32).astype(jnp.bfloat16)
        kept_keys.append(key_value[:, :HEAD_DIM])
        kept_values.append(key_value[:, HEAD_DIM:])
        new_keys = jnp.stack(kept_keys, axis=1)
        new_values = jnp.stack(kept_values, axis=1)
        heads_view = query.reshape(blocks, block_rows, HEADS, HEAD_DIM)

        def one_block(packed):
            return attend(*packed)
        mixed = lax.map(one_block, (heads_view, cache_keys.reshape(blocks, block_rows, CACHE, HEAD_DIM), cache_values.reshape(blocks, block_rows, CACHE, HEAD_DIM), lengths.reshape(blocks, block_rows), new_keys.reshape(blocks, block_rows, section + 1, HEAD_DIM), new_values.reshape(blocks, block_rows, section + 1, HEAD_DIM)))
        mixed = mixed.reshape(BATCH, HEADS * HEAD_DIM)
        results.append(grouped_output(mixed, w_out))
    return jnp.stack(results, axis=0)
```

```python
import functools
import jax
import jax.numpy as jnp
from jax import lax
from jax.experimental import pallas as pl
from jax.experimental.pallas import tpu as pltpu
from jax.sharding import PartitionSpec as P

HEAD_DIM = 256
STEPS = 2


def attend_kernel(lens_ref, q_ref, kv_ref, k_ref, v_ref, o_ref, q_f, o_f):
    r = pl.program_id(0)
    rows = pl.num_programs(0)
    local = k_ref.shape[1]
    n = q_ref.shape[0] // 4

    @pl.when(r == 0)
    def _():
        q_f[0] = q_ref[:, :128].astype(jnp.float32)
        q_f[1] = q_ref[:, 128:].astype(jnp.float32)

    picked = pl.ds(r, n, stride=4)
    q = jnp.concatenate([q_f[0, picked, :], q_f[1, picked, :]], axis=1).astype(jnp.bfloat16)
    factor = HEAD_DIM ** (-0.5)
    s = lax.dot_general(
        q, k_ref[0], (((1,), (1,)), ((), ())), preferred_element_type=jnp.float32
    ) * factor
    pos = lax.broadcasted_iota(jnp.int32, s.shape, 1)
    s = jnp.where(pos < lens_ref[r], s, -1e30)
    kv = kv_ref[...].astype(jnp.float32)
    row_id = lax.broadcasted_iota(jnp.int32, kv.shape, 0)
    fresh = [
        jnp.sum(jnp.where(row_id == t * 4 + r, kv, 0.0), axis=0, keepdims=True)
        for t in range(STEPS)
    ]
    q32 = q.astype(jnp.float32)
    new = [
        jnp.sum(q32 * fresh[t][:, :HEAD_DIM], axis=1, keepdims=True) * factor
        for t in range(STEPS)
    ]
    step = lax.broadcasted_iota(jnp.int32, (n, 1), 0) % STEPS
    for t in range(1, STEPS):
        new[t] = jnp.where(step >= t, new[t], -1e30)
    top = jnp.max(s, axis=1, keepdims=True)
    for t in range(STEPS):
        top = jnp.maximum(top, new[t])
    e = jnp.exp(s - top)
    total = jnp.sum(e, axis=1, keepdims=True)
    e_new = [jnp.exp(x - top) for x in new]
    for x in e_new:
        total = total + x
    inv = 1.0 / total
    w = (e * inv).astype(jnp.bfloat16)
    out = jnp.dot(w, v_ref[0], preferred_element_type=jnp.float32)
    for t in range(STEPS):
        wt = (e_new[t] * inv).astype(jnp.bfloat16).astype(jnp.float32)
        out = out + wt * fresh[t][:, HEAD_DIM:]
    o_f[0, picked, :] = out[:, :128]
    o_f[1, picked, :] = out[:, 128:]

    @pl.when(r == rows - 1)
    def _():
        o_ref[:, :128] = o_f[0].astype(jnp.bfloat16)
        o_ref[:, 128:] = o_f[1].astype(jnp.bfloat16)


def attend(lens, q, kv, keys, values):
    rows, cache, dim = keys.shape
    whole = lambda a: pl.BlockSpec(a.shape, lambda r: (0, 0))
    return pl.pallas_call(
        attend_kernel,
        grid=(rows,),
        out_shape=jax.ShapeDtypeStruct(q.shape, jnp.bfloat16),
        in_specs=[
            pl.BlockSpec(memory_space=pltpu.SMEM),
            whole(q),
            whole(kv),
            pl.BlockSpec((1, cache, dim), lambda r: (r, 0, 0)),
            pl.BlockSpec((1, cache, dim), lambda r: (r, 0, 0)),
        ],
        out_specs=whole(q),
        scratch_shapes=[
            pltpu.VMEM((2, q.shape[0], 128), jnp.float32),
            pltpu.VMEM((2, q.shape[0], 128), jnp.float32),
        ],
        compiler_params=pltpu.CompilerParams(vmem_limit_bytes=40 * 2**20),
    )(lens, q, kv, keys, values)


def per_device(d, n_gx, n_gy, tokens, norm_gain, w_query, w_kv, w_out, keys, values, lengths):
    local = keys.shape[0]
    pack = STEPS * local
    heads = w_query.shape[1] // HEAD_DIM
    width = tokens.shape[2]
    flats = tokens.shape[1] // local
    x = tokens.reshape(STEPS, flats, local, width).transpose(1, 0, 2, 3)
    x = x.reshape(flats * pack, width).astype(jnp.float32)
    sums, squares = lax.psum((jnp.sum(x, axis=-1), jnp.sum(x * x, axis=-1)), "gx")
    average = sums / d
    spread = squares / d - average * average
    normed = (x - average[:, None]) * lax.rsqrt(spread[:, None] + 1e-05) * norm_gain[None, :]
    normed = lax.all_gather(normed.astype(jnp.bfloat16), "gy", axis=0, tiled=True)
    q = jnp.dot(normed, w_query, preferred_element_type=jnp.float32)
    q = lax.psum_scatter(q, "gx", scatter_dimension=0, tiled=True).astype(jnp.bfloat16)
    mine = lax.dynamic_index_in_dim(
        normed.reshape(n_gx, n_gy, pack, width), lax.axis_index("gy"), 1, keepdims=False
    )
    kv = jnp.dot(mine.reshape(n_gx * pack, width), w_kv, preferred_element_type=jnp.float32)
    kv = lax.psum_scatter(kv, "gx", scatter_dimension=0, tiled=True).astype(jnp.bfloat16)
    q = q.reshape(n_gy, pack, heads, HEAD_DIM).transpose(0, 2, 1, 3)
    q = q.reshape(n_gy, heads * pack, HEAD_DIM)
    q = lax.all_to_all(q, "gy", split_axis=0, concat_axis=0, tiled=True)
    mixed = attend(lengths, q.reshape(-1, HEAD_DIM), kv, keys, values)
    mixed = mixed.reshape(n_gy, heads * pack, HEAD_DIM)
    mixed = lax.all_to_all(mixed, "gy", split_axis=0, concat_axis=0, tiled=True)
    mixed = lax.all_gather(mixed, "gx", axis=0, tiled=True)
    mixed = mixed.reshape(n_gx * n_gy, heads, pack, HEAD_DIM).transpose(0, 2, 1, 3)
    mixed = mixed.reshape(n_gx * n_gy * pack, heads * HEAD_DIM)
    out = jnp.dot(mixed, w_out, preferred_element_type=jnp.float32).astype(jnp.bfloat16)
    out = lax.psum_scatter(out, "gy", scatter_dimension=0, tiled=True)
    out = out.reshape(flats, STEPS, local, width).transpose(1, 0, 2, 3)
    return out.reshape(STEPS, flats * local, width)


def solution(mesh):
    n_gx, n_gy = mesh.shape["gx"], mesh.shape["gy"]
    in_specs = (
        P(None, "gy", "gx"),
        P("gx"),
        P("gx", "gy"),
        P("gx", None),
        P("gy", "gx"),
        P(("gx", "gy"), None, None),
        P(("gx", "gy"), None, None),
        P(("gx", "gy")),
    )

    def run(tokens, norm_gain, *rest):
        d = tokens.shape[2]
        return jax.shard_map(
            functools.partial(per_device, d, n_gx, n_gy),
            mesh=mesh, in_specs=in_specs, out_specs=P(None, "gy", "gx"), check_vma=False,
        )(tokens, norm_gain, *rest)

    return run
```

```python
import functools
import jax
import jax.numpy as jnp
from jax import lax
from jax.experimental import pallas as pl
from jax.experimental.pallas import tpu as pltpu
from jax.sharding import PartitionSpec as P

HEAD_DIM = 256
STEPS = 2


def attend_kernel(lens_ref, q_ref, kv_ref, k_ref, v_ref, o_ref, q_f, o_f):
    r = pl.program_id(0)
    rows = pl.num_programs(0)
    local = k_ref.shape[1]
    n = q_ref.shape[0] // 4

    @pl.when(r == 0)
    def _():
        q_f[0] = q_ref[:, :128].astype(jnp.float32)
        q_f[1] = q_ref[:, 128:].astype(jnp.float32)

    picked = pl.ds(r, n, stride=4)
    q = jnp.concatenate([q_f[0, picked, :], q_f[1, picked, :]], axis=1).astype(jnp.bfloat16)
    factor = HEAD_DIM ** (-0.5)
    s = lax.dot_general(
        q, k_ref[0], (((1,), (1,)), ((), ())), preferred_element_type=jnp.float32
    ) * factor
    pos = lax.broadcasted_iota(jnp.int32, s.shape, 1)
    s = jnp.where(pos < lens_ref[r], s, -1e30)
    kv = kv_ref[...].astype(jnp.float32)
    row_id = lax.broadcasted_iota(jnp.int32, kv.shape, 0)
    fresh = [
        jnp.sum(jnp.where(row_id == t * 4 + r, kv, 0.0), axis=0, keepdims=True)
        for t in range(STEPS)
    ]
    q32 = q.astype(jnp.float32)
    new = [
        jnp.sum(q32 * fresh[t][:, :HEAD_DIM], axis=1, keepdims=True) * factor
        for t in range(STEPS)
    ]
    step = lax.broadcasted_iota(jnp.int32, (n, 1), 0) % STEPS
    for t in range(1, STEPS):
        new[t] = jnp.where(step >= t, new[t], -1e30)
    top = jnp.max(s, axis=1, keepdims=True)
    for t in range(STEPS):
        top = jnp.maximum(top, new[t])
    e = jnp.exp(s - top)
    total = jnp.sum(e, axis=1, keepdims=True)
    e_new = [jnp.exp(x - top) for x in new]
    for x in e_new:
        total = total + x
    inv = 1.0 / total
    w = (e * inv).astype(jnp.bfloat16)
    out = jnp.dot(w, v_ref[0], preferred_element_type=jnp.float32)
    for t in range(STEPS):
        wt = (e_new[t] * inv).astype(jnp.bfloat16).astype(jnp.float32)
        out = out + wt * fresh[t][:, HEAD_DIM:]
    o_f[0, picked, :] = out[:, :128]
    o_f[1, picked, :] = out[:, 128:]

    @pl.when(r == rows - 1)
    def _():
        o_ref[:, :128] = o_f[0].astype(jnp.bfloat16)
        o_ref[:, 128:] = o_f[1].astype(jnp.bfloat16)


def attend(lens, q, kv, keys, values):
    rows, cache, dim = keys.shape
    whole = lambda a: pl.BlockSpec(a.shape, lambda r: (0, 0))
    return pl.pallas_call(
        attend_kernel,
        grid=(rows,),
        out_shape=jax.ShapeDtypeStruct(q.shape, jnp.bfloat16),
        in_specs=[
            pl.BlockSpec(memory_space=pltpu.SMEM),
            whole(q),
            whole(kv),
            pl.BlockSpec((1, cache, dim), lambda r: (r, 0, 0)),
            pl.BlockSpec((1, cache, dim), lambda r: (r, 0, 0)),
        ],
        out_specs=whole(q),
        scratch_shapes=[
            pltpu.VMEM((2, q.shape[0], 128), jnp.float32),
            pltpu.VMEM((2, q.shape[0], 128), jnp.float32),
        ],
        compiler_params=pltpu.CompilerParams(vmem_limit_bytes=40 * 2**20),
    )(lens, q, kv, keys, values)


MESH = pl.DeviceIdType.MESH
NT = 9


def turn(i, n):
    return lax.rem(i + 2 * n, n)


def remote(src, dst, send, recv, target):
    return pltpu.make_async_remote_copy(
        src_ref=src, dst_ref=dst, send_sem=send, recv_sem=recv,
        device_id=target, device_id_type=MESH,
    )


def greet(gx, gy, n_gx, n_gy):
    barrier = pltpu.get_barrier_semaphore()
    for o in range(1, n_gx):
        pl.semaphore_signal(
            barrier, inc=1, device_id=(turn(gx + o, n_gx), gy), device_id_type=MESH
        )
    for o in range(1, n_gy):
        pl.semaphore_signal(
            barrier, inc=1, device_id=(gx, turn(gy + o, n_gy)), device_id_type=MESH
        )
    pl.semaphore_wait(barrier, n_gx + n_gy - 2)


def project_kernel(
    d, n_gx, n_gy,
    tok_ref, gain_ref, wq_hbm, wkv_hbm, q_ref, kv_ref,
    wq, wkv, x, xg, xkv, stats, acc, own, pb, rb, kvp, kvr, qa, qb, qr,
    wq_sem, wkv_sem, st_s, st_r, ag_s, ag_r, sb_s, sb_r, fw_s, fw_r,
    kv_s, kv_r, rs_s, rs_r, aa_s, aa_r,
):
    gx, gy = lax.axis_index("gx"), lax.axis_index("gy")
    heads = wq.shape[0]
    pack = kv_ref.shape[0]
    local = pack // STEPS
    flats = x.shape[0] // pack
    block = n_gy * pack
    width = x.shape[1]
    half = n_gy // 2
    sib = gy + 1 - 2 * lax.rem(gy, 2)

    def load_q(h):
        return pltpu.make_async_copy(
            wq_hbm.at[:, pl.ds(h * HEAD_DIM, HEAD_DIM)], wq.at[h], wq_sem.at[h]
        )

    load_kv = pltpu.make_async_copy(wkv_hbm, wkv, wkv_sem)
    load_kv.start()
    for h in range(heads):
        load_q(h).start()
    greet(gx, gy, n_gx, n_gy)

    for s in range(STEPS):
        t = tok_ref[s].astype(jnp.float32)
        for f in range(flats):
            x[f * pack + s * local : f * pack + (s + 1) * local, :] = t[f * local : (f + 1) * local]
    v = x[...]
    lane = lax.broadcasted_iota(jnp.int32, stats.shape[1:], 1)
    stats[gx] = jnp.where(
        lane < 64,
        jnp.sum(v, axis=1, keepdims=True),
        jnp.sum(v * v, axis=1, keepdims=True),
    )
    sends = []
    for o in range(1, n_gx):
        c = remote(
            stats.at[gx], stats.at[gx], st_s.at[o], st_r.at[o], (turn(gx + o, n_gx), gy)
        )
        c.start()
        sends.append(c)
    for o in range(1, n_gx):
        src = turn(gx - o, n_gx)
        remote(stats.at[src], stats.at[src], st_s.at[o], st_r.at[o], (src, gy)).wait_recv()
    total = stats[0]
    for g in range(1, n_gx):
        total = total + stats[g]
    average = total[:, 0:1] / d
    spread = total[:, 64:65] / d - average * average
    normed = (x[...] - average) * lax.rsqrt(spread + 1e-05) * gain_ref[...]
    xg[gy] = normed.astype(jnp.bfloat16)

    for o in range(1, half):
        c = remote(
            xg.at[gy], xg.at[gy], ag_s.at[o], ag_r.at[o], (gx, turn(gy + 2 * o, n_gy))
        )
        c.start()
        sends.append(c)
    c = remote(xg.at[gy], xg.at[gy], sb_s, sb_r, (gx, sib))
    c.start()
    sends.append(c)
    for o in range(1, half):
        src = turn(gy - 2 * o, n_gy)
        remote(xg.at[src], xg.at[src], ag_s.at[o], ag_r.at[o], (gx, src)).wait_recv()
        c = remote(xg.at[src], xg.at[src], fw_s.at[o], fw_r.at[o], (gx, sib))
        c.start()
        sends.append(c)
    remote(xg.at[sib], xg.at[sib], sb_s, sb_r, (gx, sib)).wait_recv()
    for o in range(1, half):
        src = turn(sib - 2 * o, n_gy)
        remote(xg.at[src], xg.at[src], fw_s.at[o], fw_r.at[o], (gx, sib)).wait_recv()

    per = n_gy // flats
    at = lax.rem(gy, flats)
    for g in range(n_gx):
        two = xg[g * per + gy // flats, pl.ds(pl.multiple_of(at // 2 * 2 * pack, 2 * pack), 2 * pack), :]
        two = two.astype(jnp.float32)
        odd = lax.rem(at, 2)
        xkv[g * pack : (g + 1) * pack, :] = jnp.where(odd == 1, two[pack:], two[:pack])
    load_kv.wait()
    kv = jnp.dot(xkv[...].astype(jnp.bfloat16), wkv[...], preferred_element_type=jnp.float32)
    for g in range(n_gx):
        kvp[g] = kv[g * pack : (g + 1) * pack]
    for o in range(1, n_gx):
        dst = turn(gx + o, n_gx)
        c = remote(kvp.at[dst], kvr.at[o], kv_s.at[o], kv_r.at[o], (dst, gy))
        c.start()
        sends.append(c)

    chunk = width // 4

    def one_head(h, carry):
        load_q(h).wait()
        for k in range(4):
            part = jnp.dot(
                xg[:, :, k * chunk : (k + 1) * chunk].reshape(-1, chunk),
                wq[h, k * chunk : (k + 1) * chunk, :],
                preferred_element_type=jnp.float32,
            )
            if k == 0:
                acc[...] = part
            else:
                acc[...] += part
        for g in range(n_gx):
            pb[g, h] = acc[g * block : (g + 1) * block, :].astype(jnp.bfloat16)
        own[h] = acc[pl.ds(pl.multiple_of(gx * block, block), block), :]
        for o in range(1, n_gx):
            dst = turn(gx + o, n_gx)
            remote(
                pb.at[dst, h], rb.at[o, h], rs_s.at[o, h], rs_r.at[o, h], (dst, gy)
            ).start()
        return carry

    lax.fori_loop(0, heads, one_head, 0)

    for h in range(heads):
        got = own[h]
        for o in range(1, n_gx):
            remote(
                pb.at[o, h], rb.at[o, h], rs_s.at[o, h], rs_r.at[o, h], (turn(gx + o, n_gx), gy)
            ).wait()
            got = got + rb[o, h].astype(jnp.float32)
        for g in range(n_gy):
            qa[g, h * pack : (h + 1) * pack, :] = got[g * pack : (g + 1) * pack]
    qb[...] = qa[...].astype(jnp.bfloat16)
    for o in range(1, n_gy):
        dst = turn(gy + o, n_gy)
        c = remote(qb.at[dst], qr.at[gy], aa_s.at[o], aa_r.at[o], (gx, dst))
        c.start()
        sends.append(c)
    qr[gy] = qb[gy]
    kv = kvp[gx]
    for o in range(1, n_gx):
        remote(
            kvp.at[o], kvr.at[o], kv_s.at[o], kv_r.at[o], (turn(gx + o, n_gx), gy)
        ).wait_recv()
        kv = kv + kvr[o]
    kv_ref[...] = kv.astype(jnp.bfloat16)
    for o in range(1, n_gy):
        src = turn(gy - o, n_gy)
        remote(qb.at[src], qr.at[src], aa_s.at[o], aa_r.at[o], (gx, src)).wait_recv()
    q_ref[...] = qr[...]
    for c in sends:
        c.wait_send()


def project(d, n_gx, n_gy, local, tokens, gain, w_query, w_kv):
    pack = STEPS * local
    heads = w_query.shape[1] // HEAD_DIM
    mine = tokens.shape[0] * tokens.shape[1]
    width = tokens.shape[2]
    block = n_gy * pack
    dma = pltpu.SemaphoreType.DMA
    bf, f32 = jnp.bfloat16, jnp.float32
    vmem = pl.BlockSpec(memory_space=pltpu.VMEM)
    return pl.pallas_call(
        functools.partial(project_kernel, d, n_gx, n_gy),
        out_shape=(
            jax.ShapeDtypeStruct((n_gy, heads * pack, HEAD_DIM), bf),
            jax.ShapeDtypeStruct((pack, w_kv.shape[1]), bf),
        ),
        in_specs=[vmem, vmem, pl.BlockSpec(memory_space=pl.ANY), pl.BlockSpec(memory_space=pl.ANY)],
        out_specs=(vmem, vmem),
        scratch_shapes=[
            pltpu.VMEM((heads, width, HEAD_DIM), bf),
            pltpu.VMEM(w_kv.shape, bf),
            pltpu.VMEM((mine, width), f32),
            pltpu.VMEM((n_gy, mine, width), bf),
            pltpu.VMEM((n_gx * pack, width), f32),
            pltpu.VMEM((n_gx, mine, 128), f32),
            pltpu.VMEM((n_gy * mine, HEAD_DIM), f32),
            pltpu.VMEM((heads, block, HEAD_DIM), f32),
            pltpu.VMEM((n_gx, heads, block, HEAD_DIM), bf),
            pltpu.VMEM((n_gx, heads, block, HEAD_DIM), bf),
            pltpu.VMEM((n_gx, pack, w_kv.shape[1]), f32),
            pltpu.VMEM((n_gx, pack, w_kv.shape[1]), f32),
            pltpu.VMEM((n_gy, heads * pack, HEAD_DIM), f32),
            pltpu.VMEM((n_gy, heads * pack, HEAD_DIM), bf),
            pltpu.VMEM((n_gy, heads * pack, HEAD_DIM), bf),
            dma((heads,)), dma,
            dma((n_gx,)), dma((n_gx,)),
            dma((n_gy // 2,)), dma((n_gy // 2,)),
            dma, dma,
            dma((n_gy // 2,)), dma((n_gy // 2,)),
            dma((n_gx,)), dma((n_gx,)),
            dma((n_gx, heads)), dma((n_gx, heads)),
            dma((n_gy,)), dma((n_gy,)),
        ],
        compiler_params=pltpu.CompilerParams(
            collective_id=0, has_side_effects=True, vmem_limit_bytes=56 * 2**20
        ),
    )(tokens, gain.reshape(1, -1), w_query, w_kv)


def output_kernel(
    n_gx, n_gy, pack,
    m_ref, w_hbm, o_ref,
    w, ab, x2f, x2b, pb, sb, keep, psum, rb, of,
    w_sem, aa_s, aa_r, ag_s, ag_r, sib_s, sib_r, rs_s, rs_r,
):
    gx, gy = lax.axis_index("gx"), lax.axis_index("gy")
    tile = w.shape[2]
    heads = m_ref.shape[1] // pack
    half = n_gy // 2
    mine = x2f.shape[0] // n_gy
    odd = lax.rem(gy, 2)
    sib = gy + 1 - 2 * odd

    def load(t):
        return pltpu.make_async_copy(
            w_hbm.at[:, pl.ds(t * tile, tile)], w.at[t], w_sem.at[t]
        )

    for t in range(NT):
        load(t).start()
    greet(gx, gy, n_gx, n_gy)

    here = gx * n_gy + gy
    sends = []
    for o in range(1, n_gy):
        dst = turn(gy + o, n_gy)
        c = remote(m_ref.at[dst], ab.at[here], aa_s.at[o], aa_r.at[o], (gx, dst))
        c.start()
        sends.append(c)
    ab[here] = m_ref[gy]
    for o in range(n_gy):
        src = turn(gy - o, n_gy)
        slot = gx * n_gy + src
        if o > 0:
            remote(ab.at[slot], ab.at[slot], aa_s.at[o], aa_r.at[o], (gx, src)).wait_recv()
        for p in range(1, n_gx):
            c = remote(
                ab.at[slot], ab.at[slot], ag_s.at[o, p], ag_r.at[o, p], (turn(gx + p, n_gx), gy)
            )
            c.start()
            sends.append(c)
    for o in range(n_gy):
        for p in range(1, n_gx):
            src = turn(gx - p, n_gx)
            slot = src * n_gy + turn(gy - o, n_gy)
            remote(
                ab.at[slot], ab.at[slot], ag_s.at[o, p], ag_r.at[o, p], (src, gy)
            ).wait_recv()

    def place(g, carry):
        got = ab[g].astype(jnp.float32)
        for h in range(heads):
            x2f[pl.ds(pl.multiple_of(g * pack, pack), pack), h * HEAD_DIM : (h + 1) * HEAD_DIM] = (
                got[h * pack : (h + 1) * pack]
            )
        return carry

    lax.fori_loop(0, n_gx * n_gy, place, 0)
    x2b[...] = x2f[...].astype(jnp.bfloat16)

    def to_sib(t):
        return remote(pb.at[t, :, 1 - odd], sb.at[t], sib_s.at[t], sib_r.at[t], (gx, sib))

    def multiply(t):
        load(t).wait()
        part = jnp.dot(x2b[...], w[t], preferred_element_type=jnp.float32).astype(jnp.bfloat16)
        pb[t] = part.reshape(half, 2, mine, tile)
        to_sib(t).start()

    def to_peer(t, o):
        dst = turn(gy + 2 * o, n_gy)
        return remote(
            psum.at[t, dst // 2], rb.at[t, o], rs_s.at[t, o], rs_r.at[t, o], (gx, dst)
        )

    def pair(t):
        to_sib(t).wait()
        both = pb[t, :, odd].astype(jnp.float32) + sb[t].astype(jnp.float32)
        psum[t] = both.astype(jnp.bfloat16)
        for o in range(1, half):
            to_peer(t, o).start()
        keep[t] = pb[t, gy // 2, odd].astype(jnp.float32) + sb[t, gy // 2].astype(jnp.float32)

    multiply(0)

    def stage(t, carry):
        multiply(t)
        pair(t - 1)
        return carry

    lax.fori_loop(1, NT, stage, 0)
    pair(NT - 1)

    local = pack // STEPS
    for t in range(NT):
        out = keep[t]
        for o in range(1, half):
            to_peer(t, o).wait()
            out = out + rb[t, o].astype(jnp.float32)
        for f in range(mine // pack):
            for s in range(STEPS):
                of[s, f * local : (f + 1) * local, t * tile : (t + 1) * tile] = (
                    out[f * pack + s * local : f * pack + (s + 1) * local]
                )
    o_ref[...] = of[...].astype(jnp.bfloat16)
    for c in sends:
        c.wait_send()


def project_out(n_gx, n_gy, local, mixed, w_out):
    pack = STEPS * local
    depth, width = w_out.shape
    tile = width // NT
    rows = n_gx * n_gy * pack
    mine = rows // n_gy
    half = n_gy // 2
    dma = pltpu.SemaphoreType.DMA
    bf, f32 = jnp.bfloat16, jnp.float32
    vmem = pl.BlockSpec(memory_space=pltpu.VMEM)
    return pl.pallas_call(
        functools.partial(output_kernel, n_gx, n_gy, pack),
        out_shape=jax.ShapeDtypeStruct((STEPS, mine // STEPS, width), bf),
        in_specs=[vmem, pl.BlockSpec(memory_space=pl.ANY)],
        out_specs=vmem,
        scratch_shapes=[
            pltpu.VMEM((NT, depth, tile), bf),
            pltpu.VMEM((n_gx * n_gy,) + mixed.shape[1:], bf),
            pltpu.VMEM((rows, depth), f32),
            pltpu.VMEM((rows, depth), bf),
            pltpu.VMEM((NT, half, 2, mine, tile), bf),
            pltpu.VMEM((NT, half, mine, tile), bf),
            pltpu.VMEM((NT, mine, tile), f32),
            pltpu.VMEM((NT, half, mine, tile), bf),
            pltpu.VMEM((NT, half, mine, tile), bf),
            pltpu.VMEM((STEPS, mine // STEPS, width), f32),
            dma((NT,)),
            dma((n_gy,)), dma((n_gy,)),
            dma((n_gy, n_gx)), dma((n_gy, n_gx)),
            dma((NT,)), dma((NT,)),
            dma((NT, half)), dma((NT, half)),
        ],
        compiler_params=pltpu.CompilerParams(
            collective_id=1, has_side_effects=True, vmem_limit_bytes=56 * 2**20
        ),
    )(mixed, w_out)


def per_device(d, n_gx, n_gy, tokens, norm_gain, w_query, w_kv, w_out, keys, values, lengths):
    local = keys.shape[0]
    q, kv = project(d, n_gx, n_gy, local, tokens, norm_gain, w_query, w_kv)
    mixed = attend(lengths, q.reshape(-1, HEAD_DIM), kv, keys, values)
    return project_out(n_gx, n_gy, local, mixed.reshape(q.shape), w_out)


def solution(mesh):
    n_gx, n_gy = mesh.shape["gx"], mesh.shape["gy"]
    in_specs = (
        P(None, "gy", "gx"),
        P("gx"),
        P("gx", "gy"),
        P("gx", None),
        P("gy", "gx"),
        P(("gx", "gy"), None, None),
        P(("gx", "gy"), None, None),
        P(("gx", "gy")),
    )

    def run(tokens, norm_gain, *rest):
        d = tokens.shape[2]
        return jax.shard_map(
            functools.partial(per_device, d, n_gx, n_gy),
            mesh=mesh, in_specs=in_specs, out_specs=P(None, "gy", "gx"), check_vma=False,
        )(tokens, norm_gain, *rest)

    return run
```

```python
import functools
import jax
import jax.numpy as jnp
from jax import lax
from jax.experimental import pallas as pl
from jax.experimental.pallas import tpu as pltpu
from jax.sharding import PartitionSpec as P

HEAD_DIM = 256
STEPS = 2


def attend_kernel(lens_ref, q_ref, kv_ref, k_ref, v_ref, o_ref, q_f, o_f):
    r = pl.program_id(0)
    rows = pl.num_programs(0)
    local = k_ref.shape[1]
    n = q_ref.shape[0] // 4

    @pl.when(r == 0)
    def _():
        q_f[0] = q_ref[:, :128].astype(jnp.float32)
        q_f[1] = q_ref[:, 128:].astype(jnp.float32)

    picked = pl.ds(r, n, stride=4)
    q = jnp.concatenate([q_f[0, picked, :], q_f[1, picked, :]], axis=1).astype(jnp.bfloat16)
    factor = HEAD_DIM ** (-0.5)
    s = lax.dot_general(
        q, k_ref[0], (((1,), (1,)), ((), ())), preferred_element_type=jnp.float32
    ) * factor
    pos = lax.broadcasted_iota(jnp.int32, s.shape, 1)
    s = jnp.where(pos < lens_ref[r], s, -1e30)
    kv = kv_ref[...].astype(jnp.float32)
    row_id = lax.broadcasted_iota(jnp.int32, kv.shape, 0)
    fresh = [
        jnp.sum(jnp.where(row_id == t * 4 + r, kv, 0.0), axis=0, keepdims=True)
        for t in range(STEPS)
    ]
    q32 = q.astype(jnp.float32)
    new = [
        jnp.sum(q32 * fresh[t][:, :HEAD_DIM], axis=1, keepdims=True) * factor
        for t in range(STEPS)
    ]
    step = lax.broadcasted_iota(jnp.int32, (n, 1), 0) % STEPS
    for t in range(1, STEPS):
        new[t] = jnp.where(step >= t, new[t], -1e30)
    top = jnp.max(s, axis=1, keepdims=True)
    for t in range(STEPS):
        top = jnp.maximum(top, new[t])
    e = jnp.exp(s - top)
    total = jnp.sum(e, axis=1, keepdims=True)
    e_new = [jnp.exp(x - top) for x in new]
    for x in e_new:
        total = total + x
    inv = 1.0 / total
    w = (e * inv).astype(jnp.bfloat16)
    out = jnp.dot(w, v_ref[0], preferred_element_type=jnp.float32)
    for t in range(STEPS):
        wt = (e_new[t] * inv).astype(jnp.bfloat16).astype(jnp.float32)
        out = out + wt * fresh[t][:, HEAD_DIM:]
    o_f[0, picked, :] = out[:, :128]
    o_f[1, picked, :] = out[:, 128:]

    @pl.when(r == rows - 1)
    def _():
        o_ref[:, :128] = o_f[0].astype(jnp.bfloat16)
        o_ref[:, 128:] = o_f[1].astype(jnp.bfloat16)


def attend(lens, q, kv, keys, values):
    rows, cache, dim = keys.shape
    whole = lambda a: pl.BlockSpec(a.shape, lambda r: (0, 0))
    return pl.pallas_call(
        attend_kernel,
        grid=(rows,),
        out_shape=jax.ShapeDtypeStruct(q.shape, jnp.bfloat16),
        in_specs=[
            pl.BlockSpec(memory_space=pltpu.SMEM),
            whole(q),
            whole(kv),
            pl.BlockSpec((1, cache, dim), lambda r: (r, 0, 0)),
            pl.BlockSpec((1, cache, dim), lambda r: (r, 0, 0)),
        ],
        out_specs=whole(q),
        scratch_shapes=[
            pltpu.VMEM((2, q.shape[0], 128), jnp.float32),
            pltpu.VMEM((2, q.shape[0], 128), jnp.float32),
        ],
        compiler_params=pltpu.CompilerParams(vmem_limit_bytes=58 * 2**20),
    )(lens, q, kv, keys, values)


MESH = pl.DeviceIdType.MESH
NT = 9


def turn(i, n):
    return lax.rem(i + 2 * n, n)


def remote(src, dst, send, recv, target):
    return pltpu.make_async_remote_copy(
        src_ref=src, dst_ref=dst, send_sem=send, recv_sem=recv,
        device_id=target, device_id_type=MESH,
    )


def greet(gx, gy, n_gx, n_gy):
    barrier = pltpu.get_barrier_semaphore()
    for o in range(1, n_gx):
        pl.semaphore_signal(
            barrier, inc=1, device_id=(turn(gx + o, n_gx), gy), device_id_type=MESH
        )
    for o in range(1, n_gy):
        pl.semaphore_signal(
            barrier, inc=1, device_id=(gx, turn(gy + o, n_gy)), device_id_type=MESH
        )
    pl.semaphore_wait(barrier, n_gx + n_gy - 2)


def project_kernel(
    d, n_gx, n_gy,
    tok_ref, gain_ref, wq_hbm, wkv_hbm, q_ref, kv_ref,
    wq, wkv, xg, xkv, stats, acc, sb, rr, rl, kvp, kvr, qa, qb, qr,
    wq_sem, wkv_sem, st_s, st_r, ag_s, ag_r, sb_s, sb_r, fw_s, fw_r,
    kv_s, kv_r, ri_s, ri_r, le_s, le_r, aa_s, aa_r,
):
    gx, gy = lax.axis_index("gx"), lax.axis_index("gy")
    heads = wq.shape[0]
    pack = kv_ref.shape[0]
    local = pack // STEPS
    width = tok_ref.shape[2]
    rows = tok_ref.shape[1]
    flats = rows // local
    block = n_gy * local
    units = STEPS * heads
    half = n_gy // 2
    sib = gy + 1 - 2 * lax.rem(gy, 2)
    last = n_gx - 1

    def load_q(h):
        return pltpu.make_async_copy(
            wq_hbm.at[:, pl.ds(h * HEAD_DIM, HEAD_DIM)], wq.at[h], wq_sem.at[h]
        )

    load_kv = pltpu.make_async_copy(wkv_hbm, wkv, wkv_sem)
    for h in range(heads):
        load_q(h).start()
    load_kv.start()
    greet(gx, gy, n_gx, n_gy)

    lane = lax.broadcasted_iota(jnp.int32, (rows, 128), 1)
    for s in range(STEPS):
        v = tok_ref[s].astype(jnp.float32)
        stats[gx, s * rows : (s + 1) * rows, :] = jnp.where(
            lane < 64,
            jnp.sum(v, axis=1, keepdims=True),
            jnp.sum(v * v, axis=1, keepdims=True),
        )
    sends = []
    for o in range(1, n_gx):
        c = remote(
            stats.at[gx], stats.at[gx], st_s.at[o], st_r.at[o], (turn(gx + o, n_gx), gy)
        )
        c.start()
        sends.append(c)
    for o in range(1, n_gx):
        src = turn(gx - o, n_gx)
        remote(stats.at[src], stats.at[src], st_s.at[o], st_r.at[o], (src, gy)).wait_recv()
    total = stats[0]
    for g in range(1, n_gx):
        total = total + stats[g]

    def to_chip(s, o):
        return remote(
            xg.at[s, gy], xg.at[s, gy], ag_s.at[s, o], ag_r.at[s, o],
            (gx, turn(gy + 2 * o, n_gy)),
        )

    def to_sib(s):
        return remote(xg.at[s, gy], xg.at[s, gy], sb_s.at[s], sb_r.at[s], (gx, sib))

    def pass_on(s, o):
        src = turn(gy - 2 * o, n_gy)
        return remote(xg.at[s, src], xg.at[s, src], fw_s.at[s, o], fw_r.at[s, o], (gx, sib))

    def relay(s):
        for o in range(1, half):
            src = turn(gy - 2 * o, n_gy)
            remote(
                xg.at[s, src], xg.at[s, src], ag_s.at[s, o], ag_r.at[s, o], (gx, src)
            ).wait_recv()
            pass_on(s, o).start()

    def arrived(s):
        remote(xg.at[s, sib], xg.at[s, sib], sb_s.at[s], sb_r.at[s], (gx, sib)).wait_recv()
        for o in range(1, half):
            src = turn(sib - 2 * o, n_gy)
            remote(
                xg.at[s, src], xg.at[s, src], fw_s.at[s, o], fw_r.at[s, o], (gx, sib)
            ).wait_recv()

    for s in range(STEPS):
        t = total[s * rows : (s + 1) * rows]
        average = t[:, 0:1] / d
        spread = t[:, 64:65] / d - average * average
        normed = (tok_ref[s].astype(jnp.float32) - average) * lax.rsqrt(spread + 1e-05)
        xg[s, gy] = (normed * gain_ref[...]).astype(jnp.bfloat16)
        for o in range(1, half):
            to_chip(s, o).start()
        to_sib(s).start()
    relay(0)
    arrived(0)

    def send_kv(o):
        dst = turn(gx + o, n_gx)
        return remote(kvp.at[dst], kvr.at[o], kv_s.at[o], kv_r.at[o], (dst, gy))

    def fresh():
        per = n_gy // flats
        at = lax.rem(gy, flats)
        for g in range(n_gx):
            for s in range(STEPS):
                all_rows = xg[s, g * per + gy // flats].astype(jnp.float32)
                picked = all_rows[:local]
                for f in range(1, flats):
                    picked = jnp.where(at == f, all_rows[f * local : (f + 1) * local], picked)
                xkv[g * pack + s * local : g * pack + (s + 1) * local, :] = picked
        load_kv.wait()
        kv = jnp.dot(xkv[...].astype(jnp.bfloat16), wkv[...], preferred_element_type=jnp.float32)
        for g in range(n_gx):
            kvp[g] = kv[g * pack : (g + 1) * pack]
        for o in range(1, n_gx):
            send_kv(o).start()

    chunk = width // 4

    def product(it):
        s = it // heads
        h = it - s * heads

        @pl.when(it == heads // 2)
        def _():
            relay(1)

        @pl.when(it == heads)
        def _():
            arrived(1)

        @pl.when(it < heads)
        def _():
            load_q(h).wait()

        for k in range(4):
            part = jnp.dot(
                xg[s, :, :, k * chunk : (k + 1) * chunk].reshape(-1, chunk),
                wq[h, k * chunk : (k + 1) * chunk, :],
                preferred_element_type=jnp.float32,
            )
            if k == 0:
                acc[...] = part
            else:
                acc[...] += part
        for g in range(n_gx):
            sb[it, g] = acc[g * block : (g + 1) * block, :]

    def go_right(u, g):
        return remote(
            sb.at[u, g], rr.at[u, g], ri_s.at[u, g], ri_r.at[u, g], (turn(gx + 1, n_gx), gy)
        )

    def go_left(u, g):
        return remote(
            sb.at[u, g], rl.at[u, g], le_s.at[u, g], le_r.at[u, g], (turn(gx - 1, n_gx), gy)
        )

    def one(it, carry):
        @pl.when(it < units)
        def _():
            product(it)

        ur = it - gx

        @pl.when((ur >= 0) & (ur < units))
        def _():
            for g in reversed(range(1, n_gx)):
                @pl.when(gx < g)
                def _():
                    @pl.when(gx > 0)
                    def _():
                        go_right(ur, g).wait_recv()
                        sb[ur, g] += rr[ur, g]

                    go_right(ur, g).start()

        ul = it - (last - gx)

        @pl.when((ul >= 0) & (ul < units))
        def _():
            for g in range(last):
                @pl.when(gx > g)
                def _():
                    @pl.when(gx < last)
                    def _():
                        go_left(ul, g).wait_recv()
                        sb[ul, g] += rl[ul, g]

                    go_left(ul, g).start()

        @pl.when(it == units)
        def _():
            fresh()

        return carry

    lax.fori_loop(0, units + last, one, 0)

    def finish(h, carry):
        got = []
        for s in range(STEPS):
            u = s * heads + h

            @pl.when(gx > 0)
            def _():
                go_right(u, gx).wait_recv()
                sb[u, gx] += rr[u, gx]

            @pl.when(gx < last)
            def _():
                go_left(u, gx).wait_recv()
                sb[u, gx] += rl[u, gx]

            got.append(sb[u, gx])
        at = pl.ds(pl.multiple_of(h * pack, pack), pack)
        for g in range(n_gy):
            qa[g, at, :] = jnp.concatenate(
                [x[g * local : (g + 1) * local] for x in got], axis=0
            )
        return carry

    lax.fori_loop(0, heads, finish, 0)
    qb[...] = qa[...].astype(jnp.bfloat16)
    for o in range(1, n_gy):
        dst = turn(gy + o, n_gy)
        c = remote(qb.at[dst], qr.at[gy], aa_s.at[o], aa_r.at[o], (gx, dst))
        c.start()
        sends.append(c)
    qr[gy] = qb[gy]
    kv = kvp[gx]
    for o in range(1, n_gx):
        send_kv(o).wait_recv()
        kv = kv + kvr[o]
    kv_ref[...] = kv.astype(jnp.bfloat16)

    def sent(u, carry):
        for g in range(n_gx):
            @pl.when(gx < g)
            def _():
                go_right(u, g).wait_send()

            @pl.when(gx > g)
            def _():
                go_left(u, g).wait_send()

        return carry

    lax.fori_loop(0, units, sent, 0)
    for o in range(1, n_gy):
        src = turn(gy - o, n_gy)
        remote(qb.at[src], qr.at[src], aa_s.at[o], aa_r.at[o], (gx, src)).wait_recv()
    q_ref[...] = qr[...]
    for s in range(STEPS):
        to_sib(s).wait_send()
        for o in range(1, half):
            to_chip(s, o).wait_send()
            pass_on(s, o).wait_send()
    for o in range(1, n_gx):
        send_kv(o).wait_send()
    for c in sends:
        c.wait_send()


def project(d, n_gx, n_gy, local, tokens, gain, w_query, w_kv):
    pack = STEPS * local
    heads = w_query.shape[1] // HEAD_DIM
    rows, width = tokens.shape[1:]
    mine = STEPS * rows
    units = STEPS * heads
    dma = pltpu.SemaphoreType.DMA
    bf, f32 = jnp.bfloat16, jnp.float32
    vmem = pl.BlockSpec(memory_space=pltpu.VMEM)
    travel = pltpu.VMEM((units, n_gx, n_gy * local, HEAD_DIM), f32)
    return pl.pallas_call(
        functools.partial(project_kernel, d, n_gx, n_gy),
        out_shape=(
            jax.ShapeDtypeStruct((n_gy, heads * pack, HEAD_DIM), bf),
            jax.ShapeDtypeStruct((pack, w_kv.shape[1]), bf),
        ),
        in_specs=[vmem, vmem, pl.BlockSpec(memory_space=pl.ANY), pl.BlockSpec(memory_space=pl.ANY)],
        out_specs=(vmem, vmem),
        scratch_shapes=[
            pltpu.VMEM((heads, width, HEAD_DIM), bf),
            pltpu.VMEM(w_kv.shape, bf),
            pltpu.VMEM((STEPS, n_gy, rows, width), bf),
            pltpu.VMEM((n_gx * pack, width), f32),
            pltpu.VMEM((n_gx, mine, 128), f32),
            pltpu.VMEM((n_gy * rows, HEAD_DIM), f32),
            travel, travel, travel,
            pltpu.VMEM((n_gx, pack, w_kv.shape[1]), f32),
            pltpu.VMEM((n_gx, pack, w_kv.shape[1]), f32),
            pltpu.VMEM((n_gy, heads * pack, HEAD_DIM), f32),
            pltpu.VMEM((n_gy, heads * pack, HEAD_DIM), bf),
            pltpu.VMEM((n_gy, heads * pack, HEAD_DIM), bf),
            dma((heads,)), dma,
            dma((n_gx,)), dma((n_gx,)),
            dma((STEPS, n_gy // 2)), dma((STEPS, n_gy // 2)),
            dma((STEPS,)), dma((STEPS,)),
            dma((STEPS, n_gy // 2)), dma((STEPS, n_gy // 2)),
            dma((n_gx,)), dma((n_gx,)),
            dma((units, n_gx)), dma((units, n_gx)),
            dma((units, n_gx)), dma((units, n_gx)),
            dma((n_gy,)), dma((n_gy,)),
        ],
        compiler_params=pltpu.CompilerParams(
            collective_id=0, has_side_effects=True, vmem_limit_bytes=56 * 2**20
        ),
    )(tokens, gain.reshape(1, -1), w_query, w_kv)


def output_kernel(
    n_gx, n_gy, pack,
    m_ref, w_hbm, o_ref,
    w, ab, x2f, x2b, pb, sb, keep, psum, rb, of,
    w_sem, aa_s, aa_r, ri_s, ri_r, le_s, le_r, sib_s, sib_r, rs_s, rs_r,
):
    gx, gy = lax.axis_index("gx"), lax.axis_index("gy")
    tile = w.shape[2]
    heads = m_ref.shape[1] // pack
    half = n_gy // 2
    mine = x2f.shape[0] // n_gy
    odd = lax.rem(gy, 2)
    sib = gy + 1 - 2 * odd

    def load(t):
        return pltpu.make_async_copy(
            w_hbm.at[:, pl.ds(t * tile, tile)], w.at[t], w_sem.at[t]
        )

    for t in range(NT):
        load(t).start()
    greet(gx, gy, n_gx, n_gy)

    here = gx * n_gy + gy
    sends = []
    for o in range(1, n_gy):
        dst = turn(gy + o, n_gy)
        c = remote(m_ref.at[dst], ab.at[here], aa_s.at[o], aa_r.at[o], (gx, dst))
        c.start()
        sends.append(c)
    ab[here] = m_ref[gy]
    last = n_gx - 1

    def right(o, e):
        slot = (gx - e) * n_gy + turn(gy - o, n_gy)
        return remote(
            ab.at[slot], ab.at[slot], ri_s.at[o, e], ri_r.at[o, e], (turn(gx + 1, n_gx), gy)
        )

    def left(o, e):
        slot = (gx + e) * n_gy + turn(gy - o, n_gy)
        return remote(
            ab.at[slot], ab.at[slot], le_s.at[o, e], le_r.at[o, e], (turn(gx - 1, n_gx), gy)
        )

    def came_right(o, e):
        slot = (gx - e) * n_gy + turn(gy - o, n_gy)
        return remote(
            ab.at[slot], ab.at[slot], ri_s.at[o, e - 1], ri_r.at[o, e - 1],
            (turn(gx - 1, n_gx), gy),
        )

    def came_left(o, e):
        slot = (gx + e) * n_gy + turn(gy - o, n_gy)
        return remote(
            ab.at[slot], ab.at[slot], le_s.at[o, e - 1], le_r.at[o, e - 1],
            (turn(gx + 1, n_gx), gy),
        )

    for e in range(n_gx):
        for o in range(n_gy):
            if e == 0 and o > 0:
                src = turn(gy - o, n_gy)
                slot = gx * n_gy + src
                remote(ab.at[slot], ab.at[slot], aa_s.at[o], aa_r.at[o], (gx, src)).wait_recv()

            @pl.when(gx >= e)
            def _():
                if e > 0:
                    came_right(o, e).wait_recv()

                @pl.when(gx < last)
                def _():
                    right(o, e).start()

            @pl.when(gx + e <= last)
            def _():
                if e > 0:
                    came_left(o, e).wait_recv()

                @pl.when(gx > 0)
                def _():
                    left(o, e).start()

    def place(g, carry):
        got = ab[g].astype(jnp.float32)
        for h in range(heads):
            x2f[pl.ds(pl.multiple_of(g * pack, pack), pack), h * HEAD_DIM : (h + 1) * HEAD_DIM] = (
                got[h * pack : (h + 1) * pack]
            )
        return carry

    lax.fori_loop(0, n_gx * n_gy, place, 0)
    x2b[...] = x2f[...].astype(jnp.bfloat16)

    def to_sib(t):
        return remote(pb.at[t, :, 1 - odd], sb.at[t], sib_s.at[t], sib_r.at[t], (gx, sib))

    def multiply(t):
        load(t).wait()
        part = jnp.dot(x2b[...], w[t], preferred_element_type=jnp.float32).astype(jnp.bfloat16)
        pb[t] = part.reshape(half, 2, mine, tile)
        to_sib(t).start()

    def to_peer(t, o):
        dst = turn(gy + 2 * o, n_gy)
        return remote(
            psum.at[t, dst // 2], rb.at[t, o], rs_s.at[t, o], rs_r.at[t, o], (gx, dst)
        )

    def pair(t):
        to_sib(t).wait()
        both = pb[t, :, odd].astype(jnp.float32) + sb[t].astype(jnp.float32)
        psum[t] = both.astype(jnp.bfloat16)
        for o in range(1, half):
            to_peer(t, o).start()
        keep[t] = pb[t, gy // 2, odd].astype(jnp.float32) + sb[t, gy // 2].astype(jnp.float32)

    multiply(0)

    def stage(t, carry):
        multiply(t)
        pair(t - 1)
        return carry

    lax.fori_loop(1, NT, stage, 0)
    pair(NT - 1)

    local = pack // STEPS
    for t in range(NT):
        out = keep[t]
        for o in range(1, half):
            to_peer(t, o).wait()
            out = out + rb[t, o].astype(jnp.float32)
        for f in range(mine // pack):
            for s in range(STEPS):
                of[s, f * local : (f + 1) * local, t * tile : (t + 1) * tile] = (
                    out[f * pack + s * local : f * pack + (s + 1) * local]
                )
    o_ref[...] = of[...].astype(jnp.bfloat16)
    for e in range(n_gx):
        for o in range(n_gy):
            @pl.when((gx >= e) & (gx < last))
            def _():
                right(o, e).wait_send()

            @pl.when((gx + e <= last) & (gx > 0))
            def _():
                left(o, e).wait_send()

    for c in sends:
        c.wait_send()


def project_out(n_gx, n_gy, local, mixed, w_out):
    pack = STEPS * local
    depth, width = w_out.shape
    tile = width // NT
    rows = n_gx * n_gy * pack
    mine = rows // n_gy
    half = n_gy // 2
    dma = pltpu.SemaphoreType.DMA
    bf, f32 = jnp.bfloat16, jnp.float32
    vmem = pl.BlockSpec(memory_space=pltpu.VMEM)
    return pl.pallas_call(
        functools.partial(output_kernel, n_gx, n_gy, pack),
        out_shape=jax.ShapeDtypeStruct((STEPS, mine // STEPS, width), bf),
        in_specs=[vmem, pl.BlockSpec(memory_space=pl.ANY)],
        out_specs=vmem,
        scratch_shapes=[
            pltpu.VMEM((NT, depth, tile), bf),
            pltpu.VMEM((n_gx * n_gy,) + mixed.shape[1:], bf),
            pltpu.VMEM((rows, depth), f32),
            pltpu.VMEM((rows, depth), bf),
            pltpu.VMEM((NT, half, 2, mine, tile), bf),
            pltpu.VMEM((NT, half, mine, tile), bf),
            pltpu.VMEM((NT, mine, tile), f32),
            pltpu.VMEM((NT, half, mine, tile), bf),
            pltpu.VMEM((NT, half, mine, tile), bf),
            pltpu.VMEM((STEPS, mine // STEPS, width), f32),
            dma((NT,)),
            dma((n_gy,)), dma((n_gy,)),
            dma((n_gy, n_gx)), dma((n_gy, n_gx)),
            dma((n_gy, n_gx)), dma((n_gy, n_gx)),
            dma((NT,)), dma((NT,)),
            dma((NT, half)), dma((NT, half)),
        ],
        compiler_params=pltpu.CompilerParams(
            collective_id=1, has_side_effects=True, vmem_limit_bytes=56 * 2**20
        ),
    )(mixed, w_out)


def per_device(d, n_gx, n_gy, tokens, norm_gain, w_query, w_kv, w_out, keys, values, lengths):
    local = keys.shape[0]
    q, kv = project(d, n_gx, n_gy, local, tokens, norm_gain, w_query, w_kv)
    mixed = attend(lengths, q.reshape(-1, HEAD_DIM), kv, keys, values)
    return project_out(n_gx, n_gy, local, mixed.reshape(q.shape), w_out)


def solution(mesh):
    n_gx, n_gy = mesh.shape["gx"], mesh.shape["gy"]
    in_specs = (
        P(None, "gy", "gx"),
        P("gx"),
        P("gx", "gy"),
        P("gx", None),
        P("gy", "gx"),
        P(("gx", "gy"), None, None),
        P(("gx", "gy"), None, None),
        P(("gx", "gy")),
    )

    def run(tokens, norm_gain, *rest):
        d = tokens.shape[2]
        return jax.shard_map(
            functools.partial(per_device, d, n_gx, n_gy),
            mesh=mesh, in_specs=in_specs, out_specs=P(None, "gy", "gx"), check_vma=False,
        )(tokens, norm_gain, *rest)

    return run
```

```python
import functools
import jax
import jax.numpy as jnp
from jax import lax
from jax.experimental import pallas as pl
from jax.experimental.pallas import tpu as pltpu
from jax.sharding import PartitionSpec as P

HEAD_DIM = 256
STEPS = 2


def attend_kernel(lens_ref, q_ref, kv_ref, k_ref, v_ref, o_ref, q_f, o_f):
    r = pl.program_id(0)
    rows = pl.num_programs(0)
    local = k_ref.shape[1]
    n = q_ref.shape[0] // 4

    @pl.when(r == 0)
    def _():
        q_f[0] = q_ref[:, :128].astype(jnp.float32)
        q_f[1] = q_ref[:, 128:].astype(jnp.float32)

    heads = n // STEPS
    q = jnp.concatenate(
        [
            jnp.concatenate(
                [q_f[c, pl.ds(t * 4 + r, heads, stride=8), :] for c in range(2)], axis=1
            )
            for t in range(STEPS)
        ],
        axis=0,
    ).astype(jnp.bfloat16)
    factor = HEAD_DIM ** (-0.5)
    s = lax.dot_general(
        q, k_ref[0], (((1,), (1,)), ((), ())), preferred_element_type=jnp.float32
    ) * factor
    pos = lax.broadcasted_iota(jnp.int32, s.shape, 1)
    s = jnp.where(pos < lens_ref[r], s, -1e30)
    kv = kv_ref[...].astype(jnp.float32)
    row_id = lax.broadcasted_iota(jnp.int32, kv.shape, 0)
    fresh = [
        jnp.sum(jnp.where(row_id == t * 4 + r, kv, 0.0), axis=0, keepdims=True)
        for t in range(STEPS)
    ]
    q32 = q.astype(jnp.float32)
    new = [
        jnp.sum(q32 * fresh[t][:, :HEAD_DIM], axis=1, keepdims=True) * factor
        for t in range(STEPS)
    ]
    step = lax.broadcasted_iota(jnp.int32, (n, 1), 0) // heads
    for t in range(1, STEPS):
        new[t] = jnp.where(step >= t, new[t], -1e30)
    top = jnp.max(s, axis=1, keepdims=True)
    for t in range(STEPS):
        top = jnp.maximum(top, new[t])
    e = jnp.exp(s - top)
    total = jnp.sum(e, axis=1, keepdims=True)
    e_new = [jnp.exp(x - top) for x in new]
    for x in e_new:
        total = total + x
    inv = 1.0 / total
    w = (e * inv).astype(jnp.bfloat16)
    out = jnp.dot(w, v_ref[0], preferred_element_type=jnp.float32)
    for t in range(STEPS):
        wt = (e_new[t] * inv).astype(jnp.bfloat16).astype(jnp.float32)
        out = out + wt * fresh[t][:, HEAD_DIM:]
    for t in range(STEPS):
        for c in range(2):
            o_f[t, pl.ds(c * 4 + r, heads, stride=8), :] = out[
                t * heads : (t + 1) * heads, c * 128 : (c + 1) * 128
            ]

    @pl.when(r == rows - 1)
    def _():
        o_ref[...] = o_f[...].astype(jnp.bfloat16)


def attend(lens, q, kv, keys, values):
    rows, cache, dim = keys.shape
    whole = lambda a: pl.BlockSpec(a.shape, lambda r: (0, 0))
    return pl.pallas_call(
        attend_kernel,
        grid=(rows,),
        out_shape=jax.ShapeDtypeStruct((STEPS, q.shape[0], 128), jnp.bfloat16),
        in_specs=[
            pl.BlockSpec(memory_space=pltpu.SMEM),
            whole(q),
            whole(kv),
            pl.BlockSpec((1, cache, dim), lambda r: (r, 0, 0)),
            pl.BlockSpec((1, cache, dim), lambda r: (r, 0, 0)),
        ],
        out_specs=pl.BlockSpec((STEPS, q.shape[0], 128), lambda r: (0, 0, 0)),
        scratch_shapes=[
            pltpu.VMEM((2, q.shape[0], 128), jnp.float32),
            pltpu.VMEM((2, q.shape[0], 128), jnp.float32),
        ],
        compiler_params=pltpu.CompilerParams(vmem_limit_bytes=58 * 2**20),
    )(lens, q, kv, keys, values)


MESH = pl.DeviceIdType.MESH
NT = 9


def turn(i, n):
    return lax.rem(i + 2 * n, n)


def remote(src, dst, send, recv, target):
    return pltpu.make_async_remote_copy(
        src_ref=src, dst_ref=dst, send_sem=send, recv_sem=recv,
        device_id=target, device_id_type=MESH,
    )


def greet(gx, gy, n_gx, n_gy):
    barrier = pltpu.get_barrier_semaphore()
    for o in range(1, n_gx):
        pl.semaphore_signal(
            barrier, inc=1, device_id=(turn(gx + o, n_gx), gy), device_id_type=MESH
        )
    for o in range(1, n_gy):
        pl.semaphore_signal(
            barrier, inc=1, device_id=(gx, turn(gy + o, n_gy)), device_id_type=MESH
        )
    pl.semaphore_wait(barrier, n_gx + n_gy - 2)


def project_kernel(
    d, n_gx, n_gy,
    tok_ref, gain_ref, wq_hbm, wkv_hbm, q_ref, kv_ref,
    wq, wkv, xg, xkv, stats, acc, sb, rr, rl, kvp, kvr, qa, qb, qr,
    wq_sem, wkv_sem, st_s, st_r, ag_s, ag_r, sb_s, sb_r, fw_s, fw_r,
    kv_s, kv_r, ri_s, ri_r, le_s, le_r, aa_s, aa_r,
):
    gx, gy = lax.axis_index("gx"), lax.axis_index("gy")
    heads = wq.shape[0]
    pack = kv_ref.shape[0]
    local = pack // STEPS
    width = tok_ref.shape[2]
    rows = tok_ref.shape[1]
    flats = rows // local
    block = n_gy * local
    units = STEPS * heads
    half = n_gy // 2
    sib = gy + 1 - 2 * lax.rem(gy, 2)
    last = n_gx - 1

    def load_q(h):
        return pltpu.make_async_copy(
            wq_hbm.at[:, pl.ds(h * HEAD_DIM, HEAD_DIM)], wq.at[h], wq_sem.at[h]
        )

    load_kv = pltpu.make_async_copy(wkv_hbm, wkv, wkv_sem)
    for h in range(heads):
        load_q(h).start()
    load_kv.start()
    greet(gx, gy, n_gx, n_gy)

    lane = lax.broadcasted_iota(jnp.int32, (rows, 128), 1)
    for s in range(STEPS):
        v = tok_ref[s].astype(jnp.float32)
        stats[gx, s * rows : (s + 1) * rows, :] = jnp.where(
            lane < 64,
            jnp.sum(v, axis=1, keepdims=True),
            jnp.sum(v * v, axis=1, keepdims=True),
        )
    sends = []
    for o in range(1, n_gx):
        c = remote(
            stats.at[gx], stats.at[gx], st_s.at[o], st_r.at[o], (turn(gx + o, n_gx), gy)
        )
        c.start()
        sends.append(c)
    for o in range(1, n_gx):
        src = turn(gx - o, n_gx)
        remote(stats.at[src], stats.at[src], st_s.at[o], st_r.at[o], (src, gy)).wait_recv()
    total = stats[0]
    for g in range(1, n_gx):
        total = total + stats[g]

    def to_chip(s, o):
        return remote(
            xg.at[s, gy], xg.at[s, gy], ag_s.at[s, o], ag_r.at[s, o],
            (gx, turn(gy + 2 * o, n_gy)),
        )

    def to_sib(s):
        return remote(xg.at[s, gy], xg.at[s, gy], sb_s.at[s], sb_r.at[s], (gx, sib))

    def pass_on(s, o):
        src = turn(gy - 2 * o, n_gy)
        return remote(xg.at[s, src], xg.at[s, src], fw_s.at[s, o], fw_r.at[s, o], (gx, sib))

    def relay(s):
        for o in range(1, half):
            src = turn(gy - 2 * o, n_gy)
            remote(
                xg.at[s, src], xg.at[s, src], ag_s.at[s, o], ag_r.at[s, o], (gx, src)
            ).wait_recv()
            pass_on(s, o).start()

    def arrived(s):
        remote(xg.at[s, sib], xg.at[s, sib], sb_s.at[s], sb_r.at[s], (gx, sib)).wait_recv()
        for o in range(1, half):
            src = turn(sib - 2 * o, n_gy)
            remote(
                xg.at[s, src], xg.at[s, src], fw_s.at[s, o], fw_r.at[s, o], (gx, sib)
            ).wait_recv()

    for s in range(STEPS):
        t = total[s * rows : (s + 1) * rows]
        average = t[:, 0:1] / d
        spread = t[:, 64:65] / d - average * average
        normed = (tok_ref[s].astype(jnp.float32) - average) * lax.rsqrt(spread + 1e-05)
        xg[s, gy] = (normed * gain_ref[...]).astype(jnp.bfloat16)
        for o in range(1, half):
            to_chip(s, o).start()
        to_sib(s).start()
    relay(0)
    arrived(0)

    def send_kv(o):
        dst = turn(gx + o, n_gx)
        return remote(kvp.at[dst], kvr.at[o], kv_s.at[o], kv_r.at[o], (dst, gy))

    def fresh():
        per = n_gy // flats
        at = lax.rem(gy, flats)
        for g in range(n_gx):
            for s in range(STEPS):
                all_rows = xg[s, g * per + gy // flats].astype(jnp.float32)
                picked = all_rows[:local]
                for f in range(1, flats):
                    picked = jnp.where(at == f, all_rows[f * local : (f + 1) * local], picked)
                xkv[g * pack + s * local : g * pack + (s + 1) * local, :] = picked
        load_kv.wait()
        kv = jnp.dot(xkv[...].astype(jnp.bfloat16), wkv[...], preferred_element_type=jnp.float32)
        for g in range(n_gx):
            kvp[g] = kv[g * pack : (g + 1) * pack]
        for o in range(1, n_gx):
            send_kv(o).start()

    chunk = width // 4

    def product(it):
        s = it // heads
        h = it - s * heads

        @pl.when(it == heads // 2)
        def _():
            relay(1)

        @pl.when(it == heads)
        def _():
            arrived(1)

        @pl.when(it < heads)
        def _():
            load_q(h).wait()

        for k in range(4):
            part = jnp.dot(
                xg[s, :, :, k * chunk : (k + 1) * chunk].reshape(-1, chunk),
                wq[h, k * chunk : (k + 1) * chunk, :],
                preferred_element_type=jnp.float32,
            )
            if k == 0:
                acc[...] = part
            else:
                acc[...] += part
        for g in range(n_gx):
            sb[it, g] = acc[g * block : (g + 1) * block, :]

    def go_right(u, g):
        return remote(
            sb.at[u, g], rr.at[u, g], ri_s.at[u, g], ri_r.at[u, g], (turn(gx + 1, n_gx), gy)
        )

    def go_left(u, g):
        return remote(
            sb.at[u, g], rl.at[u, g], le_s.at[u, g], le_r.at[u, g], (turn(gx - 1, n_gx), gy)
        )

    def one(it, carry):
        @pl.when(it < units)
        def _():
            product(it)

        ur = it - 2 * gx

        @pl.when((ur >= 0) & (ur < units))
        def _():
            for g in reversed(range(1, n_gx)):
                @pl.when(gx < g)
                def _():
                    @pl.when(gx > 0)
                    def _():
                        go_right(ur, g).wait_recv()
                        sb[ur, g] += rr[ur, g]

                    go_right(ur, g).start()

        ul = it - 2 * (last - gx)

        @pl.when((ul >= 0) & (ul < units))
        def _():
            for g in range(last):
                @pl.when(gx > g)
                def _():
                    @pl.when(gx < last)
                    def _():
                        go_left(ul, g).wait_recv()
                        sb[ul, g] += rl[ul, g]

                    go_left(ul, g).start()

        @pl.when(it == units)
        def _():
            fresh()

        return carry

    lax.fori_loop(0, units + 2 * last, one, 0)

    def finish(h, carry):
        got = []
        for s in range(STEPS):
            u = s * heads + h

            @pl.when(gx > 0)
            def _():
                go_right(u, gx).wait_recv()
                sb[u, gx] += rr[u, gx]

            @pl.when(gx < last)
            def _():
                go_left(u, gx).wait_recv()
                sb[u, gx] += rl[u, gx]

            got.append(sb[u, gx])
        at = pl.ds(pl.multiple_of(h * pack, pack), pack)
        for g in range(n_gy):
            qa[g, at, :] = jnp.concatenate(
                [x[g * local : (g + 1) * local] for x in got], axis=0
            )
        return carry

    lax.fori_loop(0, heads, finish, 0)
    qb[...] = qa[...].astype(jnp.bfloat16)
    for o in range(1, n_gy):
        dst = turn(gy + o, n_gy)
        c = remote(qb.at[dst], qr.at[gy], aa_s.at[o], aa_r.at[o], (gx, dst))
        c.start()
        sends.append(c)
    qr[gy] = qb[gy]
    kv = kvp[gx]
    for o in range(1, n_gx):
        send_kv(o).wait_recv()
        kv = kv + kvr[o]
    kv_ref[...] = kv.astype(jnp.bfloat16)

    def sent(u, carry):
        for g in range(n_gx):
            @pl.when(gx < g)
            def _():
                go_right(u, g).wait_send()

            @pl.when(gx > g)
            def _():
                go_left(u, g).wait_send()

        return carry

    lax.fori_loop(0, units, sent, 0)
    for o in range(1, n_gy):
        src = turn(gy - o, n_gy)
        remote(qb.at[src], qr.at[src], aa_s.at[o], aa_r.at[o], (gx, src)).wait_recv()
    q_ref[...] = qr[...]
    for s in range(STEPS):
        to_sib(s).wait_send()
        for o in range(1, half):
            to_chip(s, o).wait_send()
            pass_on(s, o).wait_send()
    for o in range(1, n_gx):
        send_kv(o).wait_send()
    for c in sends:
        c.wait_send()


def project(d, n_gx, n_gy, local, tokens, gain, w_query, w_kv):
    pack = STEPS * local
    heads = w_query.shape[1] // HEAD_DIM
    rows, width = tokens.shape[1:]
    mine = STEPS * rows
    units = STEPS * heads
    dma = pltpu.SemaphoreType.DMA
    bf, f32 = jnp.bfloat16, jnp.float32
    vmem = pl.BlockSpec(memory_space=pltpu.VMEM)
    travel = pltpu.VMEM((units, n_gx, n_gy * local, HEAD_DIM), f32)
    return pl.pallas_call(
        functools.partial(project_kernel, d, n_gx, n_gy),
        out_shape=(
            jax.ShapeDtypeStruct((n_gy, heads * pack, HEAD_DIM), bf),
            jax.ShapeDtypeStruct((pack, w_kv.shape[1]), bf),
        ),
        in_specs=[vmem, vmem, pl.BlockSpec(memory_space=pl.ANY), pl.BlockSpec(memory_space=pl.ANY)],
        out_specs=(vmem, vmem),
        scratch_shapes=[
            pltpu.VMEM((heads, width, HEAD_DIM), bf),
            pltpu.VMEM(w_kv.shape, bf),
            pltpu.VMEM((STEPS, n_gy, rows, width), bf),
            pltpu.VMEM((n_gx * pack, width), f32),
            pltpu.VMEM((n_gx, mine, 128), f32),
            pltpu.VMEM((n_gy * rows, HEAD_DIM), f32),
            travel, travel, travel,
            pltpu.VMEM((n_gx, pack, w_kv.shape[1]), f32),
            pltpu.VMEM((n_gx, pack, w_kv.shape[1]), f32),
            pltpu.VMEM((n_gy, heads * pack, HEAD_DIM), f32),
            pltpu.VMEM((n_gy, heads * pack, HEAD_DIM), bf),
            pltpu.VMEM((n_gy, heads * pack, HEAD_DIM), bf),
            dma((heads,)), dma,
            dma((n_gx,)), dma((n_gx,)),
            dma((STEPS, n_gy // 2)), dma((STEPS, n_gy // 2)),
            dma((STEPS,)), dma((STEPS,)),
            dma((STEPS, n_gy // 2)), dma((STEPS, n_gy // 2)),
            dma((n_gx,)), dma((n_gx,)),
            dma((units, n_gx)), dma((units, n_gx)),
            dma((units, n_gx)), dma((units, n_gx)),
            dma((n_gy,)), dma((n_gy,)),
        ],
        compiler_params=pltpu.CompilerParams(
            collective_id=0, has_side_effects=True, vmem_limit_bytes=56 * 2**20
        ),
    )(tokens, gain.reshape(1, -1), w_query, w_kv)


def output_kernel(
    n_gx, n_gy, local,
    m_ref, w_hbm, o_ref,
    w, ab, x2f, x2b, pb, sb, keep, psum, rb,
    w_sem, aa_s, aa_r, ag_s, ag_r, sib_s, sib_r, rs_s, rs_r,
):
    gx, gy = lax.axis_index("gx"), lax.axis_index("gy")
    tile = w.shape[2]
    pieces = m_ref.shape[2] // local
    half = n_gy // 2
    mine = o_ref.shape[1]
    units = STEPS * NT
    odd = lax.rem(gy, 2)
    sib = gy + 1 - 2 * odd

    def load(t):
        return pltpu.make_async_copy(
            w_hbm.at[:, pl.ds(t * tile, tile)], w.at[t], w_sem.at[t]
        )

    for t in range(NT):
        load(t).start()
    greet(gx, gy, n_gx, n_gy)

    here = gx * n_gy + gy
    sends = []
    for s in range(STEPS):
        for o in range(1, n_gy):
            dst = turn(gy + o, n_gy)
            c = remote(
                m_ref.at[s, dst], ab.at[s, here], aa_s.at[s, o], aa_r.at[s, o], (gx, dst)
            )
            c.start()
            sends.append(c)
        ab[s, here] = m_ref[s, gy]
    for s in range(STEPS):
        for o in range(n_gy):
            src = turn(gy - o, n_gy)
            slot = ab.at[s, gx * n_gy + src]
            if o > 0:
                remote(slot, slot, aa_s.at[s, o], aa_r.at[s, o], (gx, src)).wait_recv()
            for p in range(1, n_gx):
                c = remote(
                    slot, slot, ag_s.at[s, o, p], ag_r.at[s, o, p], (turn(gx + p, n_gx), gy)
                )
                c.start()
                sends.append(c)

    def gathered(s):
        for o in range(n_gy):
            for p in range(1, n_gx):
                src = turn(gx - p, n_gx)
                slot = ab.at[s, src * n_gy + turn(gy - o, n_gy)]
                remote(slot, slot, ag_s.at[s, o, p], ag_r.at[s, o, p], (src, gy)).wait_recv()

        def place(g, carry):
            got = [ab[s, 2 * g + k].astype(jnp.float32) for k in range(2)]
            at = pl.ds(pl.multiple_of(g * 2 * local, 2 * local), 2 * local)
            for k in range(pieces):
                x2f[at, k * 128 : (k + 1) * 128] = jnp.concatenate(
                    [y[k * local : (k + 1) * local] for y in got], axis=0
                )
            return carry

        lax.fori_loop(0, n_gx * n_gy // 2, place, 0)
        x2b[s] = x2f[...].astype(jnp.bfloat16)

    def to_sib(u):
        return remote(pb.at[u, :, 1 - odd], sb.at[u], sib_s.at[u], sib_r.at[u], (gx, sib))

    def multiply(u):
        s = u // NT
        t = u - s * NT
        part = jnp.dot(x2b[s], w[t], preferred_element_type=jnp.float32).astype(jnp.bfloat16)
        pb[u] = part.reshape(half, 2, mine, tile)
        to_sib(u).start()

    def to_peer(u, o):
        dst = turn(gy + 2 * o, n_gy)
        return remote(
            psum.at[u, dst // 2], rb.at[u, o], rs_s.at[u, o], rs_r.at[u, o], (gx, dst)
        )

    def pair(u):
        to_sib(u).wait()
        both = pb[u, :, odd].astype(jnp.float32) + sb[u].astype(jnp.float32)
        psum[u] = both.astype(jnp.bfloat16)
        for o in range(1, half):
            to_peer(u, o).start()
        keep[u] = pb[u, gy // 2, odd].astype(jnp.float32) + sb[u, gy // 2].astype(jnp.float32)

    gathered(0)
    for u in range(2):
        load(u).wait()
        multiply(u)

    def stage(u, carry):
        pair(u - 2)

        @pl.when(u == NT)
        def _():
            gathered(1)

        @pl.when(u < NT)
        def _():
            load(u).wait()

        multiply(u)
        return carry

    lax.fori_loop(2, units, stage, 0)
    pair(units - 2)
    pair(units - 1)

    for u in range(units):
        out = keep[u]
        for o in range(1, half):
            to_peer(u, o).wait()
            out = out + rb[u, o].astype(jnp.float32)
        t = u % NT
        o_ref[u // NT, :, t * tile : (t + 1) * tile] = out.astype(jnp.bfloat16)
    for c in sends:
        c.wait_send()


def project_out(n_gx, n_gy, local, mixed, w_out):
    depth, width = w_out.shape
    tile = width // NT
    rows = n_gx * n_gy * local
    mine = rows // n_gy
    half = n_gy // 2
    units = STEPS * NT
    dma = pltpu.SemaphoreType.DMA
    bf, f32 = jnp.bfloat16, jnp.float32
    vmem = pl.BlockSpec(memory_space=pltpu.VMEM)
    return pl.pallas_call(
        functools.partial(output_kernel, n_gx, n_gy, local),
        out_shape=jax.ShapeDtypeStruct((STEPS, mine, width), bf),
        in_specs=[vmem, pl.BlockSpec(memory_space=pl.ANY)],
        out_specs=vmem,
        scratch_shapes=[
            pltpu.VMEM((NT, depth, tile), bf),
            pltpu.VMEM((STEPS, n_gx * n_gy) + mixed.shape[2:], bf),
            pltpu.VMEM((rows, depth), f32),
            pltpu.VMEM((STEPS, rows, depth), bf),
            pltpu.VMEM((units, half, 2, mine, tile), bf),
            pltpu.VMEM((units, half, mine, tile), bf),
            pltpu.VMEM((units, mine, tile), f32),
            pltpu.VMEM((units, half, mine, tile), bf),
            pltpu.VMEM((units, half, mine, tile), bf),
            dma((NT,)),
            dma((STEPS, n_gy)), dma((STEPS, n_gy)),
            dma((STEPS, n_gy, n_gx)), dma((STEPS, n_gy, n_gx)),
            dma((units,)), dma((units,)),
            dma((units, half)), dma((units, half)),
        ],
        compiler_params=pltpu.CompilerParams(
            collective_id=1, has_side_effects=True, vmem_limit_bytes=56 * 2**20
        ),
    )(mixed, w_out)


def per_device(d, n_gx, n_gy, tokens, norm_gain, w_query, w_kv, w_out, keys, values, lengths):
    local = keys.shape[0]
    q, kv = project(d, n_gx, n_gy, local, tokens, norm_gain, w_query, w_kv)
    mixed = attend(lengths, q.reshape(-1, HEAD_DIM), kv, keys, values)
    return project_out(n_gx, n_gy, local, mixed.reshape(STEPS, n_gy, -1, 128), w_out)


def solution(mesh):
    n_gx, n_gy = mesh.shape["gx"], mesh.shape["gy"]
    in_specs = (
        P(None, "gy", "gx"),
        P("gx"),
        P("gx", "gy"),
        P("gx", None),
        P("gy", "gx"),
        P(("gx", "gy"), None, None),
        P(("gx", "gy"), None, None),
        P(("gx", "gy")),
    )

    def run(tokens, norm_gain, *rest):
        d = tokens.shape[2]
        return jax.shard_map(
            functools.partial(per_device, d, n_gx, n_gy),
            mesh=mesh, in_specs=in_specs, out_specs=P(None, "gy", "gx"), check_vma=False,
        )(tokens, norm_gain, *rest)

    return run
```

```python
import functools
import jax
import jax.numpy as jnp
from jax import lax
from jax.experimental import pallas as pl
from jax.experimental.pallas import tpu as pltpu
from jax.sharding import PartitionSpec as P

HEAD_DIM = 256
STEPS = 2


def attend_kernel(lens_ref, q_ref, kv_ref, k_ref, v_ref, o_ref, q_f, o_f):
    r = pl.program_id(0)
    rows = pl.num_programs(0)
    local = k_ref.shape[1]
    n = q_ref.shape[0] // 4

    @pl.when(r == 0)
    def _():
        q_f[0] = q_ref[:, :128].astype(jnp.float32)
        q_f[1] = q_ref[:, 128:].astype(jnp.float32)

    heads = n // STEPS
    q = jnp.concatenate(
        [
            jnp.concatenate(
                [q_f[c, pl.ds(t * 4 + r, heads, stride=8), :] for c in range(2)], axis=1
            )
            for t in range(STEPS)
        ],
        axis=0,
    ).astype(jnp.bfloat16)
    factor = HEAD_DIM ** (-0.5)
    s = lax.dot_general(
        q, k_ref[0], (((1,), (1,)), ((), ())), preferred_element_type=jnp.float32
    ) * factor
    pos = lax.broadcasted_iota(jnp.int32, s.shape, 1)
    s = jnp.where(pos < lens_ref[r], s, -1e30)
    kv = kv_ref[...].astype(jnp.float32)
    row_id = lax.broadcasted_iota(jnp.int32, kv.shape, 0)
    fresh = [
        jnp.sum(jnp.where(row_id == t * 4 + r, kv, 0.0), axis=0, keepdims=True)
        for t in range(STEPS)
    ]
    q32 = q.astype(jnp.float32)
    new = [
        jnp.sum(q32 * fresh[t][:, :HEAD_DIM], axis=1, keepdims=True) * factor
        for t in range(STEPS)
    ]
    step = lax.broadcasted_iota(jnp.int32, (n, 1), 0) // heads
    for t in range(1, STEPS):
        new[t] = jnp.where(step >= t, new[t], -1e30)
    top = jnp.max(s, axis=1, keepdims=True)
    for t in range(STEPS):
        top = jnp.maximum(top, new[t])
    e = jnp.exp(s - top)
    total = jnp.sum(e, axis=1, keepdims=True)
    e_new = [jnp.exp(x - top) for x in new]
    for x in e_new:
        total = total + x
    inv = 1.0 / total
    w = (e * inv).astype(jnp.bfloat16)
    out = jnp.dot(w, v_ref[0], preferred_element_type=jnp.float32)
    for t in range(STEPS):
        wt = (e_new[t] * inv).astype(jnp.bfloat16).astype(jnp.float32)
        out = out + wt * fresh[t][:, HEAD_DIM:]
    for t in range(STEPS):
        for c in range(2):
            o_f[t, pl.ds(c * 4 + r, heads, stride=8), :] = out[
                t * heads : (t + 1) * heads, c * 128 : (c + 1) * 128
            ]

    @pl.when(r == rows - 1)
    def _():
        o_ref[...] = o_f[...].astype(jnp.bfloat16)


def attend(lens, q, kv, keys, values):
    rows, cache, dim = keys.shape
    whole = lambda a: pl.BlockSpec(a.shape, lambda r: (0, 0))
    return pl.pallas_call(
        attend_kernel,
        grid=(rows,),
        out_shape=jax.ShapeDtypeStruct((STEPS, q.shape[0], 128), jnp.bfloat16),
        in_specs=[
            pl.BlockSpec(memory_space=pltpu.SMEM),
            whole(q),
            whole(kv),
            pl.BlockSpec((1, cache, dim), lambda r: (r, 0, 0)),
            pl.BlockSpec((1, cache, dim), lambda r: (r, 0, 0)),
        ],
        out_specs=pl.BlockSpec((STEPS, q.shape[0], 128), lambda r: (0, 0, 0)),
        scratch_shapes=[
            pltpu.VMEM((2, q.shape[0], 128), jnp.float32),
            pltpu.VMEM((2, q.shape[0], 128), jnp.float32),
        ],
        compiler_params=pltpu.CompilerParams(vmem_limit_bytes=58 * 2**20),
    )(lens, q, kv, keys, values)


MESH = pl.DeviceIdType.MESH
NT = 9


def turn(i, n):
    return lax.rem(i + 2 * n, n)


def remote(src, dst, send, recv, target):
    return pltpu.make_async_remote_copy(
        src_ref=src, dst_ref=dst, send_sem=send, recv_sem=recv,
        device_id=target, device_id_type=MESH,
    )


def greet(gx, gy, n_gx, n_gy):
    barrier = pltpu.get_barrier_semaphore()
    for o in range(1, n_gx):
        pl.semaphore_signal(
            barrier, inc=1, device_id=(turn(gx + o, n_gx), gy), device_id_type=MESH
        )
    for o in range(1, n_gy):
        pl.semaphore_signal(
            barrier, inc=1, device_id=(gx, turn(gy + o, n_gy)), device_id_type=MESH
        )
    pl.semaphore_wait(barrier, n_gx + n_gy - 2)


def project_kernel(
    d, n_gx, n_gy,
    tok_ref, gain_ref, wq_hbm, wkv_hbm, q_ref, kv_ref,
    wq, wkv, xg, xkv, stats, acc, sb, rr, rl, kvp, kvr, qa, qb, qr,
    wq_sem, wkv_sem, st_s, st_r, ag_s, ag_r, sb_s, sb_r, fw_s, fw_r,
    kv_s, kv_r, ri_s, ri_r, le_s, le_r, aa_s, aa_r,
):
    gx, gy = lax.axis_index("gx"), lax.axis_index("gy")
    heads = wq.shape[0]
    pack = kv_ref.shape[0]
    local = pack // STEPS
    width = tok_ref.shape[2]
    rows = tok_ref.shape[1]
    flats = rows // local
    block = n_gy * local
    units = STEPS * heads
    half = n_gy // 2
    sib = gy + 1 - 2 * lax.rem(gy, 2)
    last = n_gx - 1

    def load_q(h):
        return pltpu.make_async_copy(
            wq_hbm.at[:, pl.ds(h * HEAD_DIM, HEAD_DIM)], wq.at[h], wq_sem.at[h]
        )

    load_kv = pltpu.make_async_copy(wkv_hbm, wkv, wkv_sem)
    for h in range(heads):
        load_q(h).start()
    load_kv.start()
    greet(gx, gy, n_gx, n_gy)

    lane = lax.broadcasted_iota(jnp.int32, (rows, 128), 1)
    for s in range(STEPS):
        v = tok_ref[s].astype(jnp.float32)
        stats[gx, s * rows : (s + 1) * rows, :] = jnp.where(
            lane < 64,
            jnp.sum(v, axis=1, keepdims=True),
            jnp.sum(v * v, axis=1, keepdims=True),
        )
    sends = []
    for o in range(1, n_gx):
        c = remote(
            stats.at[gx], stats.at[gx], st_s.at[o], st_r.at[o], (turn(gx + o, n_gx), gy)
        )
        c.start()
        sends.append(c)
    for o in range(1, n_gx):
        src = turn(gx - o, n_gx)
        remote(stats.at[src], stats.at[src], st_s.at[o], st_r.at[o], (src, gy)).wait_recv()
    total = stats[0]
    for g in range(1, n_gx):
        total = total + stats[g]

    def to_chip(s, o):
        return remote(
            xg.at[s, gy], xg.at[s, gy], ag_s.at[s, o], ag_r.at[s, o],
            (gx, turn(gy + 2 * o, n_gy)),
        )

    def to_sib(s):
        return remote(xg.at[s, gy], xg.at[s, gy], sb_s.at[s], sb_r.at[s], (gx, sib))

    def share(s):
        for o in range(1, half):
            to_chip(s, o).start()
        to_sib(s).start()

    def pass_on(s, o):
        src = turn(gy - 2 * o, n_gy)
        return remote(xg.at[s, src], xg.at[s, src], fw_s.at[s, o], fw_r.at[s, o], (gx, sib))

    def relay(s):
        for o in range(1, half):
            src = turn(gy - 2 * o, n_gy)
            remote(
                xg.at[s, src], xg.at[s, src], ag_s.at[s, o], ag_r.at[s, o], (gx, src)
            ).wait_recv()
            pass_on(s, o).start()

    def arrived(s):
        remote(xg.at[s, sib], xg.at[s, sib], sb_s.at[s], sb_r.at[s], (gx, sib)).wait_recv()
        for o in range(1, half):
            src = turn(sib - 2 * o, n_gy)
            remote(
                xg.at[s, src], xg.at[s, src], fw_s.at[s, o], fw_r.at[s, o], (gx, sib)
            ).wait_recv()

    for s in range(STEPS):
        t = total[s * rows : (s + 1) * rows]
        average = t[:, 0:1] / d
        spread = t[:, 64:65] / d - average * average
        normed = (tok_ref[s].astype(jnp.float32) - average) * lax.rsqrt(spread + 1e-05)
        xg[s, gy] = (normed * gain_ref[...]).astype(jnp.bfloat16)
        if s == 0:
            share(0)
    relay(0)
    arrived(0)
    share(1)

    def send_kv(o):
        dst = turn(gx + o, n_gx)
        return remote(kvp.at[dst], kvr.at[o], kv_s.at[o], kv_r.at[o], (dst, gy))

    def fresh():
        per = n_gy // flats
        at = lax.rem(gy, flats)
        for g in range(n_gx):
            for s in range(STEPS):
                all_rows = xg[s, g * per + gy // flats].astype(jnp.float32)
                picked = all_rows[:local]
                for f in range(1, flats):
                    picked = jnp.where(at == f, all_rows[f * local : (f + 1) * local], picked)
                xkv[g * pack + s * local : g * pack + (s + 1) * local, :] = picked
        load_kv.wait()
        kv = jnp.dot(xkv[...].astype(jnp.bfloat16), wkv[...], preferred_element_type=jnp.float32)
        for g in range(n_gx):
            kvp[g] = kv[g * pack : (g + 1) * pack]
        for o in range(1, n_gx):
            send_kv(o).start()

    chunk = width // 4

    def product(it):
        s = it // heads
        h = it - s * heads

        @pl.when(it == heads // 2)
        def _():
            relay(1)

        @pl.when(it == heads)
        def _():
            arrived(1)

        @pl.when(it < heads)
        def _():
            load_q(h).wait()

        for k in range(4):
            part = jnp.dot(
                xg[s, :, :, k * chunk : (k + 1) * chunk].reshape(-1, chunk),
                wq[h, k * chunk : (k + 1) * chunk, :],
                preferred_element_type=jnp.float32,
            )
            if k == 0:
                acc[...] = part
            else:
                acc[...] += part
        for g in range(n_gx):
            sb[it, g] = acc[g * block : (g + 1) * block, :]

    def go_right(u, g):
        return remote(
            sb.at[u, g], rr.at[u, g], ri_s.at[u, g], ri_r.at[u, g], (turn(gx + 1, n_gx), gy)
        )

    def go_left(u, g):
        return remote(
            sb.at[u, g], rl.at[u, g], le_s.at[u, g], le_r.at[u, g], (turn(gx - 1, n_gx), gy)
        )

    def one(it, carry):
        @pl.when(it < units)
        def _():
            product(it)

        ur = it - 2 * gx

        @pl.when((ur >= 0) & (ur < units))
        def _():
            for g in reversed(range(1, n_gx)):
                @pl.when(gx < g)
                def _():
                    @pl.when(gx > 0)
                    def _():
                        go_right(ur, g).wait_recv()
                        sb[ur, g] += rr[ur, g]

                    go_right(ur, g).start()

        ul = it - 2 * (last - gx)

        @pl.when((ul >= 0) & (ul < units))
        def _():
            for g in range(last):
                @pl.when(gx > g)
                def _():
                    @pl.when(gx < last)
                    def _():
                        go_left(ul, g).wait_recv()
                        sb[ul, g] += rl[ul, g]

                    go_left(ul, g).start()

        @pl.when(it == heads + 1)
        def _():
            fresh()

        return carry

    lax.fori_loop(0, units + 2 * last, one, 0)

    def finish(h, carry):
        got = []
        for s in range(STEPS):
            u = s * heads + h

            @pl.when(gx > 0)
            def _():
                go_right(u, gx).wait_recv()
                sb[u, gx] += rr[u, gx]

            @pl.when(gx < last)
            def _():
                go_left(u, gx).wait_recv()
                sb[u, gx] += rl[u, gx]

            got.append(sb[u, gx])
        at = pl.ds(pl.multiple_of(h * pack, pack), pack)
        for g in range(n_gy):
            qa[g, at, :] = jnp.concatenate(
                [x[g * local : (g + 1) * local] for x in got], axis=0
            )
        return carry

    lax.fori_loop(0, heads, finish, 0)
    qb[...] = qa[...].astype(jnp.bfloat16)
    for o in range(1, n_gy):
        dst = turn(gy + o, n_gy)
        c = remote(qb.at[dst], qr.at[gy], aa_s.at[o], aa_r.at[o], (gx, dst))
        c.start()
        sends.append(c)
    qr[gy] = qb[gy]
    kv = kvp[gx]
    for o in range(1, n_gx):
        send_kv(o).wait_recv()
        kv = kv + kvr[o]
    kv_ref[...] = kv.astype(jnp.bfloat16)

    def sent(u, carry):
        for g in range(n_gx):
            @pl.when(gx < g)
            def _():
                go_right(u, g).wait_send()

            @pl.when(gx > g)
            def _():
                go_left(u, g).wait_send()

        return carry

    lax.fori_loop(0, units, sent, 0)
    for o in range(1, n_gy):
        src = turn(gy - o, n_gy)
        remote(qb.at[src], qr.at[src], aa_s.at[o], aa_r.at[o], (gx, src)).wait_recv()
    q_ref[...] = qr[...]
    for s in range(STEPS):
        to_sib(s).wait_send()
        for o in range(1, half):
            to_chip(s, o).wait_send()
            pass_on(s, o).wait_send()
    for o in range(1, n_gx):
        send_kv(o).wait_send()
    for c in sends:
        c.wait_send()


def project(d, n_gx, n_gy, local, tokens, gain, w_query, w_kv):
    pack = STEPS * local
    heads = w_query.shape[1] // HEAD_DIM
    rows, width = tokens.shape[1:]
    mine = STEPS * rows
    units = STEPS * heads
    dma = pltpu.SemaphoreType.DMA
    bf, f32 = jnp.bfloat16, jnp.float32
    vmem = pl.BlockSpec(memory_space=pltpu.VMEM)
    travel = pltpu.VMEM((units, n_gx, n_gy * local, HEAD_DIM), f32)
    return pl.pallas_call(
        functools.partial(project_kernel, d, n_gx, n_gy),
        out_shape=(
            jax.ShapeDtypeStruct((n_gy, heads * pack, HEAD_DIM), bf),
            jax.ShapeDtypeStruct((pack, w_kv.shape[1]), bf),
        ),
        in_specs=[vmem, vmem, pl.BlockSpec(memory_space=pl.ANY), pl.BlockSpec(memory_space=pl.ANY)],
        out_specs=(vmem, vmem),
        scratch_shapes=[
            pltpu.VMEM((heads, width, HEAD_DIM), bf),
            pltpu.VMEM(w_kv.shape, bf),
            pltpu.VMEM((STEPS, n_gy, rows, width), bf),
            pltpu.VMEM((n_gx * pack, width), f32),
            pltpu.VMEM((n_gx, mine, 128), f32),
            pltpu.VMEM((n_gy * rows, HEAD_DIM), f32),
            travel, travel, travel,
            pltpu.VMEM((n_gx, pack, w_kv.shape[1]), f32),
            pltpu.VMEM((n_gx, pack, w_kv.shape[1]), f32),
            pltpu.VMEM((n_gy, heads * pack, HEAD_DIM), f32),
            pltpu.VMEM((n_gy, heads * pack, HEAD_DIM), bf),
            pltpu.VMEM((n_gy, heads * pack, HEAD_DIM), bf),
            dma((heads,)), dma,
            dma((n_gx,)), dma((n_gx,)),
            dma((STEPS, n_gy // 2)), dma((STEPS, n_gy // 2)),
            dma((STEPS,)), dma((STEPS,)),
            dma((STEPS, n_gy // 2)), dma((STEPS, n_gy // 2)),
            dma((n_gx,)), dma((n_gx,)),
            dma((units, n_gx)), dma((units, n_gx)),
            dma((units, n_gx)), dma((units, n_gx)),
            dma((n_gy,)), dma((n_gy,)),
        ],
        compiler_params=pltpu.CompilerParams(
            collective_id=0, has_side_effects=True, vmem_limit_bytes=56 * 2**20
        ),
    )(tokens, gain.reshape(1, -1), w_query, w_kv)


def output_kernel(
    n_gx, n_gy, local,
    m_ref, w_hbm, o_ref,
    w, ab, x2f, x2b, pb, sb, keep, psum, rb,
    w_sem, aa_s, aa_r, ag_s, ag_r, sib_s, sib_r, rs_s, rs_r,
):
    gx, gy = lax.axis_index("gx"), lax.axis_index("gy")
    tile = w.shape[2]
    pieces = m_ref.shape[2] // local
    half = n_gy // 2
    mine = o_ref.shape[1]
    units = STEPS * NT
    odd = lax.rem(gy, 2)
    sib = gy + 1 - 2 * odd

    def load(t):
        return pltpu.make_async_copy(
            w_hbm.at[:, pl.ds(t * tile, tile)], w.at[t], w_sem.at[t]
        )

    for t in range(NT):
        load(t).start()
    greet(gx, gy, n_gx, n_gy)

    here = gx * n_gy + gy
    sends = []
    for s in range(STEPS):
        for o in range(1, n_gy):
            dst = turn(gy + o, n_gy)
            c = remote(
                m_ref.at[s, dst], ab.at[s, here], aa_s.at[s, o], aa_r.at[s, o], (gx, dst)
            )
            c.start()
            sends.append(c)
        ab[s, here] = m_ref[s, gy]
    def pass_along(s):
        for o in range(n_gy):
            src = turn(gy - o, n_gy)
            slot = ab.at[s, gx * n_gy + src]
            if o > 0:
                remote(slot, slot, aa_s.at[s, o], aa_r.at[s, o], (gx, src)).wait_recv()
            for p in range(1, n_gx):
                c = remote(
                    slot, slot, ag_s.at[s, o, p], ag_r.at[s, o, p], (turn(gx + p, n_gx), gy)
                )
                c.start()
                sends.append(c)

    def landed(s):
        for o in range(n_gy):
            for p in range(1, n_gx):
                src = turn(gx - p, n_gx)
                slot = ab.at[s, src * n_gy + turn(gy - o, n_gy)]
                remote(slot, slot, ag_s.at[s, o, p], ag_r.at[s, o, p], (src, gy)).wait_recv()

    def gathered(s):
        def place(g, carry):
            got = [ab[s, 2 * g + k].astype(jnp.float32) for k in range(2)]
            at = pl.ds(pl.multiple_of(g * 2 * local, 2 * local), 2 * local)
            for k in range(pieces):
                x2f[at, k * 128 : (k + 1) * 128] = jnp.concatenate(
                    [y[k * local : (k + 1) * local] for y in got], axis=0
                )
            return carry

        lax.fori_loop(0, n_gx * n_gy // 2, place, 0)
        x2b[s] = x2f[...].astype(jnp.bfloat16)

    def to_sib(u):
        return remote(pb.at[u, :, 1 - odd], sb.at[u], sib_s.at[u], sib_r.at[u], (gx, sib))

    def multiply(u):
        s = u // NT
        t = u - s * NT
        part = jnp.dot(x2b[s], w[t], preferred_element_type=jnp.float32).astype(jnp.bfloat16)
        pb[u] = part.reshape(half, 2, mine, tile)
        to_sib(u).start()

    def to_peer(u, o):
        dst = turn(gy + 2 * o, n_gy)
        return remote(
            psum.at[u, dst // 2], rb.at[u, o], rs_s.at[u, o], rs_r.at[u, o], (gx, dst)
        )

    def pair(u):
        to_sib(u).wait()
        both = pb[u, :, odd].astype(jnp.float32) + sb[u].astype(jnp.float32)
        psum[u] = both.astype(jnp.bfloat16)
        for o in range(1, half):
            to_peer(u, o).start()
        keep[u] = pb[u, gy // 2, odd].astype(jnp.float32) + sb[u, gy // 2].astype(jnp.float32)

    pass_along(0)
    landed(0)
    pass_along(1)
    gathered(0)
    for u in range(2):
        load(u).wait()
        multiply(u)

    def stage(u, carry):
        pair(u - 2)

        @pl.when(u == NT)
        def _():
            landed(1)
            gathered(1)

        @pl.when(u < NT)
        def _():
            load(u).wait()

        multiply(u)
        return carry

    lax.fori_loop(2, units, stage, 0)
    pair(units - 2)
    pair(units - 1)

    for u in range(units):
        out = keep[u]
        for o in range(1, half):
            to_peer(u, o).wait()
            out = out + rb[u, o].astype(jnp.float32)
        t = u % NT
        o_ref[u // NT, :, t * tile : (t + 1) * tile] = out.astype(jnp.bfloat16)
    for c in sends:
        c.wait_send()


def project_out(n_gx, n_gy, local, mixed, w_out):
    depth, width = w_out.shape
    tile = width // NT
    rows = n_gx * n_gy * local
    mine = rows // n_gy
    half = n_gy // 2
    units = STEPS * NT
    dma = pltpu.SemaphoreType.DMA
    bf, f32 = jnp.bfloat16, jnp.float32
    vmem = pl.BlockSpec(memory_space=pltpu.VMEM)
    return pl.pallas_call(
        functools.partial(output_kernel, n_gx, n_gy, local),
        out_shape=jax.ShapeDtypeStruct((STEPS, mine, width), bf),
        in_specs=[vmem, pl.BlockSpec(memory_space=pl.ANY)],
        out_specs=vmem,
        scratch_shapes=[
            pltpu.VMEM((NT, depth, tile), bf),
            pltpu.VMEM((STEPS, n_gx * n_gy) + mixed.shape[2:], bf),
            pltpu.VMEM((rows, depth), f32),
            pltpu.VMEM((STEPS, rows, depth), bf),
            pltpu.VMEM((units, half, 2, mine, tile), bf),
            pltpu.VMEM((units, half, mine, tile), bf),
            pltpu.VMEM((units, mine, tile), f32),
            pltpu.VMEM((units, half, mine, tile), bf),
            pltpu.VMEM((units, half, mine, tile), bf),
            dma((NT,)),
            dma((STEPS, n_gy)), dma((STEPS, n_gy)),
            dma((STEPS, n_gy, n_gx)), dma((STEPS, n_gy, n_gx)),
            dma((units,)), dma((units,)),
            dma((units, half)), dma((units, half)),
        ],
        compiler_params=pltpu.CompilerParams(
            collective_id=1, has_side_effects=True, vmem_limit_bytes=56 * 2**20
        ),
    )(mixed, w_out)


def per_device(d, n_gx, n_gy, tokens, norm_gain, w_query, w_kv, w_out, keys, values, lengths):
    local = keys.shape[0]
    q, kv = project(d, n_gx, n_gy, local, tokens, norm_gain, w_query, w_kv)
    mixed = attend(lengths, q.reshape(-1, HEAD_DIM), kv, keys, values)
    return project_out(n_gx, n_gy, local, mixed.reshape(STEPS, n_gy, -1, 128), w_out)


def solution(mesh):
    n_gx, n_gy = mesh.shape["gx"], mesh.shape["gy"]
    in_specs = (
        P(None, "gy", "gx"),
        P("gx"),
        P("gx", "gy"),
        P("gx", None),
        P("gy", "gx"),
        P(("gx", "gy"), None, None),
        P(("gx", "gy"), None, None),
        P(("gx", "gy")),
    )

    def run(tokens, norm_gain, *rest):
        d = tokens.shape[2]
        return jax.shard_map(
            functools.partial(per_device, d, n_gx, n_gy),
            mesh=mesh, in_specs=in_specs, out_specs=P(None, "gy", "gx"), check_vma=False,
        )(tokens, norm_gain, *rest)

    return run
```
